32 devices in a mesh: ops: 8 (over y, x, core), sec: 4 (over z).
Axes of the slice: x: 2, y: 2, z: 4, core: 2. Of those that a mesh axis runs over, the one named last changes fastest.
Arguments:
- wavefunction: float32 [8, 128, 128], P('sec'), may hold values from -6 to 6
- hamiltonian_diag: float32 [8, 128, 128], P('sec'), may hold values from -6 to 6
- mirror_coupling: float32 [8], P('sec'), may hold values from 0.5 to 1.5, as said below
- left_env: float32 [192, 8, 128, 128], P('ops', 'sec'), as said below
- right_env: float32 [192, 128, 128], P('ops'), as said below
- term_source: int32 [192, 8], P('ops', 'sec'), may hold values from -1 to 7, as said below
Outputs:
- new_wave: float32 [8, 128, 128], P('sec', 'ops')
- new_sigma: float32 [8, 128, 128], P('sec', 'ops')
- energy: float32 [1], replicated
The draws below stay inside these ranges and needn't reach their ends.
Inputs may be any that keep to these rules, and one draw needn't show every extreme that they name: `term_source`: for each term the non-negative entries over the 8 target sectors are distinct; terms 0 and 1 have a block for every sector; for even k, term k + 1 maps sector t into sector s exactly where term k maps s into t. For even k and term_source[k, s] = t >= 0, left_env[k + 1, t] is the transpose of left_env[k, s]. For even k, right_env[k + 1] is the transpose of right_env[k]. mirror_coupling[s] equals mirror_coupling[s + 4].
All inputs are finite; a program needn't handle non-finite values.
Results may differ from the reference program's by a relative error of at most 0.0003.
Values sent between devices are 32-bit elements; how exact they have to be, the bound alone decides.
No kernel may reach another device: no remote copies, remote signals or barrier semaphores. Data moves between devices by JAX's collectives and lax.ppermute only.
A program may use at most 64 MiB of HBM per device.

```python
import jax
import jax.numpy as jnp
from jax import lax

B = 128
TERMS_DEV = 24
S = 8
TERMS = 192
N_OPS = 8


def paired_tables(key):
    keys = jax.random.split(jax.random.fold_in(key, 7), 6)
    half_terms = TERMS // 2
    orders = jax.vmap(lambda item: jax.random.permutation(item, S))(jax.random.split(keys[0], half_terms))
    level = jax.random.randint(keys[1], (S,), 1, 8)
    empty_sector = jax.random.randint(keys[2], (), 0, S)
    level = jnp.where(jnp.arange(S) == empty_sector, 0, level)
    trials = jax.random.randint(keys[3], (half_terms, S), 0, 8)
    active = (trials < level[None, :]) | (jnp.arange(half_terms)[:, None] == 0)
    inverse = jnp.argsort(orders, axis=1, stable=True).astype(jnp.int32)
    back_active = jnp.take_along_axis(active, inverse, axis=1)
    forward = jnp.where(active, orders, -1)
    backward = jnp.where(back_active, inverse, -1)
    source = jnp.stack([forward, backward], axis=1).reshape(TERMS, S).astype(jnp.int32)
    left_half = jax.random.normal(keys[4], (half_terms, S, B, B), jnp.float32) * (B * TERMS) ** (-0.5)
    left_back = jnp.swapaxes(left_half[jnp.arange(half_terms)[:, None], inverse], 2, 3)
    left = jnp.stack([left_half, left_back], axis=1).reshape(TERMS, S, B, B)
    right_half = jax.random.normal(keys[5], (half_terms, B, B), jnp.float32) * B ** (-0.5)
    right = jnp.stack([right_half, jnp.swapaxes(right_half, 1, 2)], axis=1).reshape(TERMS, B, B)
    return (source, left, right)


def draw_term_source(key, part):
    return paired_tables(key)[0]


def draw_left_env(key, part):
    return paired_tables(key)[1]


def draw_right_env(key, part):
    return paired_tables(key)[2]


def draw_mirror_coupling(key, part):
    half_values = jax.random.uniform(jax.random.fold_in(key, 11), (S // 2,), jnp.float32, 0.5, 1.5)
    return jnp.concatenate([half_values, half_values])


def shard_levels(rng, dims, cuts, least, top_value):
    gain, own = 1.0, jax.random.fold_in(rng, 6)
    for axis_at, blocks in cuts:
        heights = jnp.exp(jax.random.uniform(jax.random.fold_in(own, axis_at), (blocks,), jnp.float32, least / len(cuts), top_value / len(cuts)))
        gain = gain * jnp.repeat(heights, dims[axis_at] // blocks).reshape([-1 if axis == axis_at else 1 for axis in range(len(dims))])
    return gain


def noise(own_key, extent, deviation, reach, cuts=(), kind=jnp.bfloat16):
    array = jax.random.normal(own_key, extent, jnp.float32) * deviation
    if len(cuts) > 0:
        array = shard_levels(own_key, extent, cuts, -0.22, 0.18) * array
    return jnp.clip(array, min=-reach, max=reach).astype(kind)


def setup_inputs(seed: int = 0) -> dict:
    streams_of = jax.random.split(jax.random.key(seed), 7)
    wavefunction = noise(streams_of[0], (S, B, B), 1.0, 6.0, ((0, 4),), jnp.float32)
    hamiltonian_diag = noise(streams_of[1], (S, B, B), 1.0, 6.0, ((0, 4),), jnp.float32)
    mirror_coupling = draw_mirror_coupling(jax.random.fold_in(streams_of[6], 71), 0)
    left_env = draw_left_env(jax.random.fold_in(streams_of[6], 71), 0)
    right_env = draw_right_env(jax.random.fold_in(streams_of[6], 71), 0)
    term_source = draw_term_source(jax.random.fold_in(streams_of[6], 71), 0)
    return {"wavefunction": wavefunction, "hamiltonian_diag": hamiltonian_diag, "mirror_coupling": mirror_coupling, "left_env": left_env, "right_env": right_env, "term_source": term_source}


HIGH = lax.Precision.HIGHEST

def apply_hamiltonian(vector, left_env, right_env, term_source, mirror_coupling):
    sectors = vector.shape[0]
    partner = jnp.roll(vector, sectors // 2, axis=0)
    mirrored = mirror_coupling[:, None, None] * jnp.swapaxes(partner, 1, 2)
    left_groups = left_env.reshape(N_OPS, TERMS_DEV, sectors, B, B)
    right_groups = right_env.reshape(N_OPS, TERMS_DEV, B, B)
    source_groups = term_source.reshape(N_OPS, TERMS_DEV, sectors)

    def group_step(total, pieces):
        left_block, right_block, source_block = pieces
        picked = vector[jnp.maximum(source_block, 0).astype(jnp.int32)]
        picked = jnp.where((source_block >= 0)[:, :, None, None], picked, jnp.zeros_like(picked))
        inner = jnp.einsum('ksij,ksjl->ksil', left_block, picked, precision=HIGH)
        outer = jnp.einsum('ksil,kml->sim', inner, right_block, precision=HIGH)
        return (total + outer, None)
    total, _ = lax.scan(group_step, jnp.zeros_like(vector), (left_groups, right_groups, source_groups))
    return total + mirrored

def reference(wavefunction, hamiltonian_diag, mirror_coupling, left_env, right_env, term_source):
    sigma = apply_hamiltonian(wavefunction, left_env, right_env, term_source, mirror_coupling)
    norm_sq = jnp.sum(wavefunction * wavefunction)
    correlation = jnp.sum(wavefunction * sigma)
    scale = jnp.sqrt(norm_sq)
    unit = wavefunction / scale
    rayleigh = correlation / norm_sq
    resid = sigma / scale - rayleigh * unit
    offset = hamiltonian_diag - rayleigh
    correction = resid / (1.0 + offset * offset)
    along = jnp.sum(unit * correction)
    correction = correction - along * unit
    direction = correction / jnp.sqrt(jnp.sum(correction * correction))
    dir_sigma = apply_hamiltonian(direction, left_env, right_env, term_source, mirror_coupling)
    coupling = jnp.sum(direction * resid)
    curvature = jnp.sum(direction * dir_sigma)
    half_gap = 0.5 * (curvature - rayleigh)
    energy = 0.5 * (rayleigh + curvature) - jnp.sqrt(half_gap * half_gap + coupling * coupling)
    angle = 0.5 * jnp.arctan2(-coupling, half_gap)
    new_wave = jnp.cos(angle) * wavefunction + jnp.sin(angle) * scale * direction
    new_sigma = jnp.cos(angle) * sigma + jnp.sin(angle) * scale * dir_sigma
    return (new_wave, new_sigma, jnp.reshape(energy, (1,)))
```

```python
import functools

import jax
import jax.numpy as jnp
from jax import lax
from jax.experimental import pallas as pl
from jax.experimental.pallas import tpu as pltpu
from jax.sharding import PartitionSpec as P

F32 = jnp.float32
BF16 = jnp.bfloat16
VMEM = pl.BlockSpec(memory_space=pltpu.VMEM)
SMEM = pl.BlockSpec(memory_space=pltpu.SMEM)
PAD = 8
LIMIT = 48 * 1024 * 1024


def call(kernel, out_shape, in_specs, scratch=(), flops=0):
    return pl.pallas_call(
        kernel,
        out_shape=out_shape,
        in_specs=in_specs,
        out_specs=jax.tree.map(lambda _: VMEM, out_shape),
        scratch_shapes=list(scratch),
        compiler_params=pltpu.CompilerParams(vmem_limit_bytes=LIMIT),
        cost_estimate=pl.CostEstimate(flops=flops, bytes_accessed=1 << 20, transcendentals=0),
    )


def split(values):
    high = values.astype(BF16)
    return high, (values - high.astype(F32)).astype(BF16)


def total(values):
    return jnp.sum(values, keepdims=True)


def store_vector(slots, at, block):
    size = block.shape[0]
    high, low = split(block)
    slots[at, :size, :size] = high
    slots[at, :size, size:] = low
    slots[at, size:, :size] = high
    slots[at, size:, size:] = jnp.zeros_like(high)


def apply_terms(source_ref, left_ref, right_ref, slots, stacked, weights, where, empty):
    terms, owned, size, _ = left_ref.shape
    for k in range(terms):
        high, low = split(right_ref[k])
        base = 2 * k * size
        weights[base : base + size, :size] = high
        weights[base : base + size, size:] = low
        weights[base + size : base + 2 * size, :size] = high
        weights[base + size : base + 2 * size, size:] = jnp.zeros_like(high)
    for k in range(terms):
        base = 2 * (k ^ 1) * size
        for s in range(owned):
            t = source_ref[k, s]
            at = jnp.where(t < 0, empty, where(jnp.maximum(t, 0)))
            pair = jnp.concatenate(split(left_ref[k, s]), axis=1)
            both = jnp.dot(pair, slots[at], preferred_element_type=F32)
            high, low = split(both[:, :size] + both[:, size:])
            stacked[s * size : (s + 1) * size, base : base + size] = high
            stacked[s * size : (s + 1) * size, base + size : base + 2 * size] = low
    both = jnp.dot(stacked[...], weights[...], preferred_element_type=F32)
    return both[:, :size] + both[:, size:]


def place(n_sec, core, plane):
    def where(t):
        return jnp.bitwise_xor(t // 2, plane) + n_sec * jnp.bitwise_xor(t % 2, core)

    return where


def first_kernel(n_sec, n_ops, source_ref, at_ref, coupling_ref, left_ref, right_ref, own_ref, other_ref,
                 out_ref, slots, stacked, weights):
    core, plane = at_ref[0], at_ref[1]
    size = own_ref.shape[1]
    where = place(n_sec, core, plane)
    for m in range(n_sec):
        store_vector(slots, m, own_ref[m])
        store_vector(slots, n_sec + m, other_ref[m])
    slots[2 * n_sec] = jnp.zeros_like(slots[2 * n_sec])
    part = apply_terms(source_ref, left_ref, right_ref, slots, stacked, weights, where, 2 * n_sec)
    mirror = jnp.bitwise_xor((plane + n_sec // 2) % n_sec, plane)
    corr = jnp.zeros((1, 1), F32)
    for s in range(2):
        mine = core == s
        partner = jnp.where(mine, own_ref[mirror], other_ref[mirror])
        vec = jnp.where(mine, own_ref[0], other_ref[0])
        block = part[s * size : (s + 1) * size] + (coupling_ref[s] / n_ops) * partner.T
        out_ref[s, :size] = block
        corr += total(vec * block)
    for s in range(2):
        out_ref[s, size:] = jnp.broadcast_to(corr, (PAD, size))


def correction_kernel(n_sec, sums_ref, own_ref, other_ref, diag_ref, out_ref, scalar_ref):
    size = own_ref.shape[1]
    norm_sq = total(own_ref[...] * own_ref[...]).reshape(1, 1) + total(other_ref[...] * other_ref[...]).reshape(1, 1)
    corr = jnp.sum(sums_ref[:, size : size + 1, :1], axis=0)
    scale = jnp.sqrt(norm_sq)
    rayleigh = corr / norm_sq
    for m in range(n_sec):
        sigma = sums_ref[m, :size]
        resid = sigma / scale - rayleigh * (own_ref[m] / scale)
        offset = diag_ref[m] - rayleigh
        out_ref[m] = resid / (1.0 + offset * offset)
    out_ref[n_sec] = sums_ref[0, :size]
    lane = lax.broadcasted_iota(jnp.int32, (PAD, size), 1)
    scalar_ref[...] = jnp.where(lane < size // 2, scale, rayleigh)


def second_kernel(n_sec, n_ops, source_ref, at_ref, coupling_ref, left_ref, right_ref, own_ref, other_ref,
                  mine_ref, theirs_ref, scalar_ref, out_ref, dir_ref, slots, stacked, weights, direction):
    core, plane = at_ref[0], at_ref[1]
    size = own_ref.shape[1]
    where = place(n_sec, core, plane)
    scale = scalar_ref[:1, :1]
    rayleigh = scalar_ref[:1, size // 2 : size // 2 + 1]
    pieces = [(mine_ref, own_ref, m) for m in range(n_sec)] + [(theirs_ref, other_ref, m) for m in range(n_sec)]
    acc = jnp.zeros((size, size), F32)
    for corr_ref, wave_ref, m in pieces:
        acc += corr_ref[m] * wave_ref[m]
    along = total(acc) / scale
    acc = jnp.zeros((size, size), F32)
    for i, (corr_ref, wave_ref, m) in enumerate(pieces):
        rest = corr_ref[m] - along * (wave_ref[m] / scale)
        direction[i] = rest
        acc += rest * rest
    norm = jnp.sqrt(total(acc))
    for i in range(2 * n_sec):
        block = direction[i] / norm
        direction[i] = block
        store_vector(slots, i, block)
    slots[2 * n_sec] = jnp.zeros_like(slots[2 * n_sec])
    part = apply_terms(source_ref, left_ref, right_ref, slots, stacked, weights, where, 2 * n_sec)
    mirror = jnp.bitwise_xor((plane + n_sec // 2) % n_sec, plane)
    curvature = jnp.zeros((1, 1), F32)
    coupling = jnp.zeros((1, 1), F32)
    rows = size // n_ops
    for s in range(2):
        mine = core == s
        at = jnp.where(mine, 0, n_sec)
        vec = direction[at]
        wave = jnp.where(mine, own_ref[0], other_ref[0])
        sigma = jnp.where(mine, mine_ref[n_sec], theirs_ref[n_sec])
        block = part[s * size : (s + 1) * size] + (coupling_ref[s] / n_ops) * direction[at + mirror].T
        dir_ref[s] = vec
        curvature += total(vec * block)
        coupling += total(vec * (sigma / scale - rayleigh * (wave / scale)))
        for o in range(n_ops):
            at_row = ((o // 2) * 2 + s) * rows
            out_ref[o % 2, at_row : at_row + rows] = block[o * rows : (o + 1) * rows]
    lane = lax.broadcasted_iota(jnp.int32, (PAD, size), 1)
    sums = jnp.where(lane < size // 2, curvature, coupling / n_ops)
    for c in range(2):
        out_ref[c, size:] = sums


def ritz_kernel(n_sec, scalar_ref, sums_ref, wave_ref, dir_ref, sigma_ref, dir_sigma_ref, wave_out, sigma_out, energy_out):
    half = scalar_ref.shape[1] // 2
    scale = scalar_ref[:1, :1]
    rayleigh = scalar_ref[:1, half : half + 1]
    sums = jnp.sum(sums_ref[...], axis=0)
    curvature = sums[:1, :1]
    coupling = sums[:1, half : half + 1]
    half_gap = 0.5 * (curvature - rayleigh)
    radius = jnp.sqrt(half_gap * half_gap + coupling * coupling)
    energy = 0.5 * (rayleigh + curvature) - radius
    safe = jnp.where(radius > 0.0, radius, 1.0)
    big = jnp.sqrt(0.5 + 0.5 * (jnp.abs(half_gap) / safe))
    small = (0.5 * (jnp.abs(coupling) / safe)) / big
    ahead = half_gap >= 0.0
    cos_part = jnp.where(radius > 0.0, jnp.where(ahead, big, small), 1.0)
    sin_size = jnp.where(radius > 0.0, jnp.where(ahead, small, big), 0.0)
    sin_part = jnp.where(coupling < 0.0, sin_size, -sin_size)
    lift = sin_part * scale
    wave_out[...] = cos_part * wave_ref[...] + lift * dir_ref[...]
    sigma_out[...] = cos_part * sigma_ref[...] + lift * dir_sigma_ref[...]
    energy_out[...] = jnp.broadcast_to(energy, energy_out.shape)


def body(n_ops, n_sec, wavefunction, hamiltonian_diag, mirror_coupling, left_env, right_env, term_source):
    owned, size, _ = wavefunction.shape
    terms = left_env.shape[0]
    chips = n_ops // 2
    rows = size // n_ops
    me_ops, me_sec = lax.axis_index("ops"), lax.axis_index("sec")
    core, chip = me_ops % 2, me_ops // 2

    def swap(values):
        return lax.ppermute(values, "ops", [(i, i ^ 1) for i in range(n_ops)])

    def to_chip(values, m):
        return lax.ppermute(values, "ops", [(i, i ^ (2 * m)) for i in range(n_ops)])

    def to_plane(values, m):
        return lax.ppermute(values, "sec", [(i, i ^ m) for i in range(n_sec)])

    def gather_planes(values):
        return jnp.stack([values] + [to_plane(values, m) for m in range(1, n_sec)])

    def pick(values, index):
        return lax.dynamic_index_in_dim(values, index, 0, keepdims=False)

    at = jnp.stack([core, me_sec]).astype(jnp.int32)
    matmul_flops = terms * owned * size * size * size * 12
    scratch = [
        pltpu.VMEM((2 * n_sec + 1, 2 * size, 2 * size), BF16),
        pltpu.VMEM((owned * size, 2 * terms * size), BF16),
        pltpu.VMEM((2 * terms * size, 2 * size), BF16),
    ]

    with jax.named_scope("gather_wave"):
        own = gather_planes(pick(wavefunction, core))
        other = jnp.concatenate([pick(wavefunction, 1 - core)[None], swap(own[1:])])
    with jax.named_scope("gather_diag"):
        diag = gather_planes(pick(hamiltonian_diag, core))

    with jax.named_scope("first_apply"):
        part = call(
            functools.partial(first_kernel, n_sec, n_ops),
            jax.ShapeDtypeStruct((owned, size + PAD, size), F32),
            [SMEM, SMEM, SMEM, VMEM, VMEM, VMEM, VMEM],
            scratch,
            matmul_flops,
        )(term_source, at, mirror_coupling, left_env, right_env, own, other)
    with jax.named_scope("reduce_sigma"):
        summed = pick(part, core) + swap(pick(part, 1 - core))
        summed = sum([to_chip(summed, m) for m in range(1, chips)], summed)
    with jax.named_scope("gather_sigma"):
        sums = gather_planes(summed)
    with jax.named_scope("correction"):
        mine, scalars = call(
            functools.partial(correction_kernel, n_sec),
            (jax.ShapeDtypeStruct((n_sec + 1, size, size), F32), jax.ShapeDtypeStruct((PAD, size), F32)),
            [VMEM] * 4,
        )(sums, own, other, diag)
        theirs = swap(mine)
    with jax.named_scope("second_apply"):
        part, direction = call(
            functools.partial(second_kernel, n_sec, n_ops),
            (
                jax.ShapeDtypeStruct((2, size + PAD, size), F32),
                jax.ShapeDtypeStruct((owned, size, size), F32),
            ),
            [SMEM, SMEM, SMEM] + [VMEM] * 7,
            scratch + [pltpu.VMEM((2 * n_sec, size, size), F32)],
            matmul_flops,
        )(term_source, at, mirror_coupling, left_env, right_env, own, other, mine, theirs, scalars)
    with jax.named_scope("reduce_dir_sigma"):
        summed = pick(part, core) + swap(pick(part, 1 - core))
        tail = summed[size:]

        def message(q):
            return jnp.concatenate([lax.dynamic_slice_in_dim(summed, q * (2 * rows), 2 * rows, 0), tail])

        got = sum([to_chip(message(chip ^ m), m) for m in range(1, chips)], message(chip))
        dir_sigma = got[: 2 * rows].reshape(owned, rows, size)
        scalar_sums = gather_planes(got[2 * rows :])
    with jax.named_scope("ritz"):
        sigma = jnp.stack([jnp.where(core == 0, mine[n_sec], theirs[n_sec]), jnp.where(core == 0, theirs[n_sec], mine[n_sec])])

        def own_rows(values):
            return lax.dynamic_slice_in_dim(values, me_ops * rows, rows, 1)

        new_wave, new_sigma, energy = call(
            functools.partial(ritz_kernel, n_sec),
            (
                jax.ShapeDtypeStruct((owned, rows, size), F32),
                jax.ShapeDtypeStruct((owned, rows, size), F32),
                jax.ShapeDtypeStruct((1, size), F32),
            ),
            [VMEM] * 6,
        )(scalars, scalar_sums, own_rows(wavefunction), own_rows(direction), own_rows(sigma), dir_sigma)
    return (new_wave, new_sigma, energy[0, :1])


def solution(mesh):
    placed = (
        P("sec", None, None),
        P("sec", None, None),
        P("sec"),
        P("ops", "sec", None, None),
        P("ops", None, None),
        P("ops", "sec"),
    )
    return jax.shard_map(
        functools.partial(body, mesh.shape["ops"], mesh.shape["sec"]),
        mesh=mesh,
        in_specs=placed,
        out_specs=(P("sec", "ops", None), P("sec", "ops", None), P()),
        check_vma=False,
    )
```

```python
import functools

import jax
import jax.numpy as jnp
from jax import lax
from jax.experimental import pallas as pl
from jax.experimental.pallas import tpu as pltpu
from jax.sharding import PartitionSpec as P

F32 = jnp.float32
BF16 = jnp.bfloat16
VMEM = pl.BlockSpec(memory_space=pltpu.VMEM)
HBM = pl.BlockSpec(memory_space=pltpu.HBM)
SMEM = pl.BlockSpec(memory_space=pltpu.SMEM)
PAD = 8
LIMIT = 32 * 1024 * 1024
SMALL = 16 * 1024 * 1024


def call(kernel, out_shape, in_specs, scratch=(), flops=0, limit=LIMIT):
    return pl.pallas_call(
        kernel,
        out_shape=out_shape,
        in_specs=in_specs,
        out_specs=jax.tree.map(lambda _: VMEM, out_shape),
        scratch_shapes=list(scratch),
        compiler_params=pltpu.CompilerParams(vmem_limit_bytes=limit),
        cost_estimate=pl.CostEstimate(flops=flops, bytes_accessed=1 << 20, transcendentals=0),
    )


def split(values):
    high = values.astype(BF16)
    return high, (values - high.astype(F32)).astype(BF16)


def total(values):
    return jnp.sum(values, keepdims=True)


def spread(value, size):
    return jnp.broadcast_to(value, (1, size))


def load_kernel(count, *refs):
    sources, targets, sems = refs[:count], refs[count : 2 * count], refs[2 * count]
    copies = [pltpu.make_async_copy(source, target, sems.at[i]) for i, (source, target) in enumerate(zip(sources, targets))]
    for copy in copies:
        copy.start()
    for copy in copies:
        copy.wait()


def pack_kernel(wave_ref, diag_ref, packed_ref, own_diag_ref, sems):
    size = wave_ref.shape[1]
    share = packed_ref.shape[0] - size
    ops = lax.axis_index("ops")
    core, chip = ops % 2, ops // 2
    first = pl.multiple_of(chip * share, share)
    copies = [
        pltpu.make_async_copy(wave_ref.at[core], packed_ref.at[pl.ds(0, size)], sems.at[0]),
        pltpu.make_async_copy(diag_ref.at[core, pl.ds(first, share)], packed_ref.at[pl.ds(size, share)], sems.at[1]),
        pltpu.make_async_copy(diag_ref.at[core], own_diag_ref, sems.at[2]),
    ]
    for copy in copies:
        copy.start()
    for copy in copies:
        copy.wait()


def store_vector(slots, at, block):
    size = block.shape[0]
    high, low = split(block)
    slots[at, :size, :size] = high
    slots[at, :size, size:] = low
    slots[at, size:, :size] = high
    slots[at, size:, size:] = jnp.zeros_like(high)


def apply_terms(n_sec, source_ref, left_ref, right_ref, slots, stacked, weights):
    terms, owned, size, _ = left_ref.shape
    plane = lax.axis_index("sec")
    slots[2 * n_sec] = jnp.zeros_like(slots[2 * n_sec])
    for k in range(terms):
        base = 2 * (k ^ 1) * size
        for s in range(owned):
            source = source_ref[s, k]
            at = 2 * jnp.bitwise_xor(source // 2, plane) + jnp.bitwise_and(source, 1)
            pair = jnp.concatenate(split(left_ref[k, s]), axis=1)
            inner = jnp.dot(pair, slots[jnp.where(source < 0, 2 * n_sec, at)], preferred_element_type=F32)
            high, low = split(inner[:, :size] + inner[:, size:])
            stacked[s * size : (s + 1) * size, base : base + size] = high
            stacked[s * size : (s + 1) * size, base + size : base + 2 * size] = low
    for k in range(terms):
        base = 2 * k * size
        high, low = split(right_ref[k])
        weights[base : base + size, :size] = high
        weights[base : base + size, size:] = low
        weights[base + size : base + 2 * size, :size] = high
        weights[base + size : base + 2 * size, size:] = jnp.zeros_like(high)
    both = jnp.dot(stacked[...], weights[...], preferred_element_type=F32)
    return both[:, :size] + both[:, size:]


def join_kernel(keep_ref, got_ref, packed_refs, out_ref):
    rows = keep_ref.shape[0]
    out_ref[:rows] = keep_ref[...] + got_ref[...]
    share = (out_ref.shape[0] - rows) // max(len(packed_refs), 1)
    for i, ref in enumerate(packed_refs):
        out_ref[rows + i * share : rows + (i + 1) * share] = ref[ref.shape[0] - share :]


def plane_kernel(part_refs, own_diag_ref, near_ref, far_ref, diag_refs):
    rows = far_ref.shape[0]
    size = own_diag_ref.shape[0]
    summed = part_refs[0][:rows]
    for ref in part_refs[1:]:
        summed += ref[:rows]
    far_ref[...] = summed
    near_ref[:rows] = summed
    near_ref[rows:] = own_diag_ref[...]
    chip = lax.axis_index("ops") // 2
    share = size // len(part_refs)
    for m, ref in enumerate(part_refs):
        first = pl.multiple_of(jnp.bitwise_xor(chip, m) * share, share)
        for i, diag_ref in enumerate(diag_refs):
            diag_ref[pl.ds(first, share)] = ref[rows + i * share : rows + (i + 1) * share]


def first_kernel(n_sec, n_ops, source_ref, coupling_ref, left_ref, right_ref, local_ref, near_ref, mine_refs, theirs_refs,
                 keep_ref, send_ref, norm_ref, slots, stacked, weights):
    size = local_ref.shape[1]
    core = lax.axis_index("ops") % 2
    acc = jnp.zeros((size, size), F32)
    for m in range(n_sec):
        for s in range(2):
            if m < 2:
                at, block = 2 * m + s, (local_ref, near_ref)[m][s]
            else:
                at, block = 2 * m + (core if s == 0 else 1 - core), (mine_refs, theirs_refs)[s][m - 2][:size]
            acc += block * block
            store_vector(slots, at, block)
    norm_ref[...] = jnp.broadcast_to(total(acc), norm_ref.shape)
    part = apply_terms(n_sec, source_ref, left_ref, right_ref, slots, stacked, weights)
    corr = jnp.zeros((1, 1), F32)
    mirror = n_sec // 2
    blocks = []
    for s in range(2):
        if mirror < 2:
            partner = near_ref[s]
        else:
            partner = jnp.where(core == s, mine_refs[mirror - 2][:size], theirs_refs[mirror - 2][:size])
        blocks.append(part[s * size : (s + 1) * size] + (coupling_ref[0, s] / n_ops) * partner.T)
        corr += total(local_ref[s] * blocks[s])
    keep_ref[:size] = jnp.where(core == 0, blocks[0], blocks[1])
    send_ref[:size] = jnp.where(core == 0, blocks[1], blocks[0])
    keep_ref[size:] = jnp.broadcast_to(corr, (PAD, size))
    send_ref[size:] = jnp.broadcast_to(corr, (PAD, size))


def correction_kernel(n_sec, norm_ref, local_ref, near_ref, mine_refs, sum_refs, own_diag_ref, diag_refs, out_ref):
    size = local_ref.shape[1]
    core = lax.axis_index("ops") % 2
    norm_sq = norm_ref[:1, :1]
    corr = sum_refs[0][size : size + 1, :1]
    for ref in sum_refs[1:]:
        corr += ref[size : size + 1, :1]
    scale = jnp.sqrt(norm_sq)
    inverse = 1.0 / scale
    rayleigh = corr / norm_sq
    sums = [jnp.zeros((size, size), F32) for _ in range(5)]
    for m in range(n_sec):
        wave = local_ref[core] if m == 0 else near_ref[core] if m == 1 else mine_refs[m - 2][:size]
        sigma = sum_refs[m][:size]
        resid = sigma * inverse - rayleigh * (wave * inverse)
        diag = own_diag_ref[...] if m == 0 else sum_refs[1][size + PAD :] if m == 1 else diag_refs[m - 2][...]
        offset = diag - rayleigh
        corrected = resid / (1.0 + offset * offset)
        out_ref[m * size : (m + 1) * size] = corrected
        for i, factor in enumerate((wave, corrected, resid, sigma)):
            sums[i] += corrected * factor
        sums[4] += wave * resid
    out_ref[n_sec * size : (n_sec + 1) * size] = sum_refs[0][:size]
    tail = [spread(scale, size), spread(rayleigh, size)] + [spread(total(values), size) for values in sums]
    for i, row in enumerate(tail):
        out_ref[(n_sec + 1) * size + i : (n_sec + 1) * size + i + 1] = row
    for i in range(len(tail), PAD):
        out_ref[(n_sec + 1) * size + i : (n_sec + 1) * size + i + 1] = jnp.zeros((1, size), F32)


def second_kernel(n_sec, n_ops, source_ref, coupling_ref, left_ref, right_ref, mine_ref, theirs_ref,
                  keep_ref, send_ref, own_ref, scalar_ref, slots, stacked, weights):
    size = left_ref.shape[2]
    core = lax.axis_index("ops") % 2
    for m in range(n_sec):
        span = pl.ds(m * size, size)
        store_vector(slots, 2 * m + core, mine_ref[span])
        store_vector(slots, 2 * m + 1 - core, theirs_ref[span])
    part = apply_terms(n_sec, source_ref, left_ref, right_ref, slots, stacked, weights)
    curvature = jnp.zeros((1, 1), F32)
    rows = size // n_ops
    mirror = pl.ds(n_sec // 2 * size, size)
    kept = pl.ds(n_sec * size, size)
    for s in range(2):
        mine = core == s
        vec = jnp.where(mine, mine_ref[:size], theirs_ref[:size])
        partner = jnp.where(mine, mine_ref[mirror], theirs_ref[mirror])
        block = part[s * size : (s + 1) * size] + (coupling_ref[0, s] / n_ops) * partner.T
        own_ref[s] = vec
        own_ref[2 + s] = jnp.where(mine, mine_ref[kept], theirs_ref[kept])
        curvature += total(vec * block)
        for q in range(n_ops // 2):
            at_row = (q * 2 + s) * rows
            even = block[2 * q * rows : (2 * q + 1) * rows]
            odd = block[(2 * q + 1) * rows : (2 * q + 2) * rows]
            keep_ref[at_row : at_row + rows] = jnp.where(core == 0, even, odd)
            send_ref[at_row : at_row + rows] = jnp.where(core == 0, odd, even)
    keep_ref[size:] = jnp.broadcast_to(curvature, (PAD, size))
    send_ref[size:] = jnp.broadcast_to(curvature, (PAD, size))
    tail = pl.ds((n_sec + 1) * size, PAD)
    row = lax.broadcasted_iota(jnp.int32, (PAD, size), 0)
    scalar_ref[...] = mine_ref[tail] + jnp.where(row < 2, 0.0, theirs_ref[tail])


def ritz_kernel(scalar_ref, wave_ref, own_ref, applied_ref, sum_refs, wave_out, sigma_out, energy_out):
    scale, rayleigh, wave_corr, corr_sq, corr_resid, corr_sigma, wave_resid = (scalar_ref[i : i + 1, :1] for i in range(7))
    curve = sum_refs[0][:1, :1]
    for ref in sum_refs[1:]:
        curve += ref[:1, :1]
    along = wave_corr / scale
    lift = along / scale
    norm_sq = corr_sq - along * along
    norm = jnp.sqrt(norm_sq)
    coupling = (corr_resid - lift * wave_resid) / norm
    curvature = (curve - 2.0 * lift * corr_sigma + along * along * rayleigh) / norm_sq
    half_gap = 0.5 * (curvature - rayleigh)
    radius = jnp.sqrt(half_gap * half_gap + coupling * coupling)
    energy = 0.5 * (rayleigh + curvature) - radius
    safe = jnp.where(radius > 0.0, radius, 1.0)
    big = jnp.sqrt(0.5 + 0.5 * (jnp.abs(half_gap) / safe))
    small = (0.5 * (jnp.abs(coupling) / safe)) / big
    ahead = half_gap >= 0.0
    cos_part = jnp.where(radius > 0.0, jnp.where(ahead, big, small), 1.0)
    sin_size = jnp.where(radius > 0.0, jnp.where(ahead, small, big), 0.0)
    sin_part = jnp.where(coupling < 0.0, sin_size, -sin_size)
    factor = sin_part * scale / norm
    wave_out[...] = cos_part * wave_ref[...] + factor * (own_ref[:2] - lift * wave_ref[...])
    sigma_out[...] = cos_part * own_ref[2:] + factor * (applied_ref[...] - lift * own_ref[2:])
    energy_out[...] = jnp.broadcast_to(energy, energy_out.shape)


def body(n_ops, n_sec, wavefunction, hamiltonian_diag, mirror_coupling, left_env, right_env, term_source):
    owned, size, _ = wavefunction.shape
    terms = left_env.shape[0]
    half = terms // 4 * 2
    chips = n_ops // 2
    rows = size // n_ops
    me_ops, me_sec = lax.axis_index("ops"), lax.axis_index("sec")
    core, chip = me_ops % 2, me_ops // 2
    shape = jax.ShapeDtypeStruct

    def swap(values):
        return lax.ppermute(values, "ops", [(i, i ^ 1) for i in range(n_ops)])

    def to_chip(values, m):
        return lax.ppermute(values, "ops", [(i, i ^ (2 * m)) for i in range(n_ops)])

    def to_plane(values, m):
        return lax.ppermute(values, "sec", [(i, i ^ m) for i in range(n_sec)])

    def gather_planes(values):
        return [values] + [to_plane(values, m) for m in range(1, n_sec)]

    def pick(values, index):
        return lax.dynamic_index_in_dim(values, index, 0, keepdims=False)

    matmul_flops = terms * owned * size * size * size * 12
    scratch = [
        pltpu.VMEM((2 * n_sec + 1, 2 * size, 2 * size), BF16),
        pltpu.VMEM((owned * size, 2 * terms * size), BF16),
        pltpu.VMEM((2 * terms * size, 2 * size), BF16),
    ]
    message_shape = shape((size + PAD, size), F32)
    scalar_shape = shape((PAD, size), F32)

    def in_hbm(values):
        return pltpu.with_memory_space_constraint(values, pltpu.HBM)

    with jax.named_scope("gather_wave"):
        near = to_plane(wavefunction, 1)
        packed, own_diag = call(
            pack_kernel,
            (shape((size + size // chips, size), F32), shape((size, size), F32)),
            [HBM] * 2,
            [pltpu.SemaphoreType.DMA((3,))],
            limit=SMALL,
        )(in_hbm(wavefunction), in_hbm(hamiltonian_diag))
        mine = [to_plane(packed, m) for m in range(2, n_sec)]
    with jax.named_scope("load"):
        held = [left_env, right_env, wavefunction, term_source.T, mirror_coupling[None]]
        loaded = call(
            functools.partial(load_kernel, len(held)),
            tuple(shape(values.shape, values.dtype) for values in held),
            [HBM] * len(held),
            [pltpu.SemaphoreType.DMA((len(held),))],
            limit=SMALL,
        )(*[in_hbm(values) for values in held])
        loaded, mine = lax.optimization_barrier((loaded, mine))
        left, right, local, source, coupling = loaded
    with jax.named_scope("swap_wave"):
        theirs = [swap(values) for values in mine]
    with jax.named_scope("first_apply"):
        keep, send, norm = call(
            functools.partial(first_kernel, n_sec, n_ops),
            (message_shape, message_shape, scalar_shape),
            [SMEM, SMEM] + [VMEM] * 4 + [[VMEM] * (n_sec - 2)] * 2,
            scratch,
            matmul_flops,
        )(source, coupling, left, right, local, near, mine, theirs)
    with jax.named_scope("reduce_sigma"):
        share = size // chips
        joined = call(
            join_kernel,
            shape((size + PAD + (n_sec - 2) * share, size), F32),
            [VMEM, VMEM, [VMEM] * (n_sec - 2)],
            limit=SMALL,
        )(keep, swap(send), mine)
        near_sum, far_sum, diag = call(
            plane_kernel,
            (shape((2 * size + PAD, size), F32), message_shape, [shape((size, size), F32)] * (n_sec - 2)),
            [[VMEM] * chips, VMEM],
            limit=SMALL,
        )([joined] + [to_chip(joined, m) for m in range(1, chips)], own_diag)
    with jax.named_scope("gather_sigma"):
        sums = [far_sum, to_plane(near_sum, 1)] + [to_plane(far_sum, m) for m in range(2, n_sec)]
    with jax.named_scope("correction"):
        found = call(
            functools.partial(correction_kernel, n_sec),
            shape(((n_sec + 1) * size + PAD, size), F32),
            [VMEM] * 3 + [[VMEM] * (n_sec - 2), [VMEM] * n_sec, VMEM, [VMEM] * (n_sec - 2)],
            limit=SMALL,
        )(norm, local, near, mine, sums, own_diag, diag)
        other = swap(found)
    with jax.named_scope("second_apply"):
        keep, send, kept, scalars = call(
            functools.partial(second_kernel, n_sec, n_ops),
            (message_shape, message_shape, shape((2 * owned, size, size), F32), scalar_shape),
            [SMEM, SMEM] + [VMEM] * 4,
            scratch,
            matmul_flops,
        )(source, coupling, left, right, found, other)
    with jax.named_scope("reduce_dir_sigma"):
        summed = keep + swap(send)
        tail = summed[size:]

        def message(q):
            return jnp.concatenate([lax.dynamic_slice_in_dim(summed, q * (2 * rows), 2 * rows, 0), tail])

        got = sum([to_chip(message(chip ^ m), m) for m in range(1, chips)], message(chip))
        applied = got[: 2 * rows].reshape(owned, rows, size)
        curves = gather_planes(got[2 * rows :])
    with jax.named_scope("ritz"):

        def own_rows(values):
            return lax.dynamic_slice_in_dim(values, me_ops * rows, rows, 1)

        new_wave, new_sigma, energy = call(
            ritz_kernel,
            (shape((owned, rows, size), F32), shape((owned, rows, size), F32), shape((1, size), F32)),
            [VMEM] * 4 + [[VMEM] * n_sec],
        )(scalars, own_rows(local), own_rows(kept), applied, curves)
    return (new_wave, new_sigma, energy[0, :1])


def solution(mesh):
    placed = (
        P("sec", None, None),
        P("sec", None, None),
        P("sec"),
        P("ops", "sec", None, None),
        P("ops", None, None),
        P("ops", "sec"),
    )
    return jax.shard_map(
        functools.partial(body, mesh.shape["ops"], mesh.shape["sec"]),
        mesh=mesh,
        in_specs=placed,
        out_specs=(P("sec", "ops", None), P("sec", "ops", None), P()),
        check_vma=False,
    )
```

```python
import functools

import jax
import jax.numpy as jnp
from jax import lax
from jax.experimental import pallas as pl
from jax.experimental.pallas import tpu as pltpu
from jax.sharding import PartitionSpec as P

F32 = jnp.float32
BF16 = jnp.bfloat16
VMEM = pl.BlockSpec(memory_space=pltpu.VMEM)
HBM = pl.BlockSpec(memory_space=pltpu.HBM)
SMEM = pl.BlockSpec(memory_space=pltpu.SMEM)
PAD = 8
LIMIT = 16 * 1024 * 1024
SMALL = 16 * 1024 * 1024


def call(kernel, out_shape, in_specs, scratch=(), flops=0, limit=LIMIT):
    return pl.pallas_call(
        kernel,
        out_shape=out_shape,
        in_specs=in_specs,
        out_specs=jax.tree.map(lambda _: VMEM, out_shape),
        scratch_shapes=list(scratch),
        compiler_params=pltpu.CompilerParams(vmem_limit_bytes=limit),
        cost_estimate=pl.CostEstimate(flops=flops, bytes_accessed=1 << 20, transcendentals=0),
    )


def split(values):
    high = values.astype(BF16)
    return high, (values - high.astype(F32)).astype(BF16)


def total(values):
    return jnp.sum(values, keepdims=True)


def spread(value, size):
    return jnp.broadcast_to(value, (1, size))


def position(k, terms):
    return k // 2 + k % 2 * (terms // 2)


def load_kernel(left_ref, right_ref, wave_ref, source_ref, coupling_ref,
                pairs_ref, weights_ref, local_ref, sources_ref, couplings_ref, left_buf, right_buf, sems):
    terms, owned, size, _ = left_ref.shape
    sources = (left_ref, right_ref, wave_ref, source_ref, coupling_ref)
    targets = (left_buf, right_buf, local_ref, sources_ref, couplings_ref)
    copies = [pltpu.make_async_copy(source, target, sems.at[i]) for i, (source, target) in enumerate(zip(sources, targets))]
    for copy in copies:
        copy.start()
    for copy in copies:
        copy.wait()
    for k in range(terms):
        for s in range(owned):
            pairs_ref[k, s, :, :size], pairs_ref[k, s, :, size:] = split(left_buf[k, s])
        base = 2 * size * position(k, terms)
        high, low = split(right_buf[k ^ 1])
        weights_ref[base : base + size, :size] = high
        weights_ref[base : base + size, size:] = low
        weights_ref[base + size : base + 2 * size, :size] = high
        weights_ref[base + size : base + 2 * size, size:] = jnp.zeros_like(high)


def pack_kernel(wave_ref, diag_ref, packed_ref, near_ref, own_diag_ref, sems):
    owned, size, _ = wave_ref.shape
    share = packed_ref.shape[0] - size
    ops = lax.axis_index("ops")
    core, chip = ops % 2, ops // 2
    rows = pl.ds(pl.multiple_of(chip * share, share), share)
    moves = [
        (wave_ref.at[core], packed_ref.at[pl.ds(0, size)]),
        (diag_ref.at[core, rows], packed_ref.at[pl.ds(size, share)]),
        *((wave_ref.at[s], near_ref.at[pl.ds(s * size, size)]) for s in range(owned)),
        (diag_ref.at[core, rows], near_ref.at[pl.ds(owned * size, share)]),
        (diag_ref.at[core], own_diag_ref),
    ]
    copies = [pltpu.make_async_copy(source, target, sems.at[i]) for i, (source, target) in enumerate(moves)]
    for copy in copies:
        copy.start()
    for copy in copies:
        copy.wait()


def store_vector(slots, at, block):
    size = block.shape[0]
    high, low = split(block)
    slots[at, :size, :size] = high
    slots[at, :size, size:] = low
    slots[at, size:, :size] = high
    slots[at, size:, size:] = jnp.zeros_like(high)


def apply_terms(chosen, n_sec, source_ref, pairs_ref, weights_ref, slots, stacked):
    terms, owned, size, _ = pairs_ref.shape
    plane = lax.axis_index("sec")
    first = position(chosen[0], terms)
    for k in chosen:
        base = 2 * size * (position(k, terms) - first)
        for s in range(owned):
            source = source_ref[s, k]
            at = 2 * jnp.bitwise_xor(source // 2, plane) + jnp.bitwise_and(source, 1)
            inner = jnp.dot(pairs_ref[k, s], slots[jnp.where(source < 0, 2 * n_sec, at)], preferred_element_type=F32)
            high, low = split(inner[:, :size] + inner[:, size:])
            stacked[s * size : (s + 1) * size, base : base + size] = high
            stacked[s * size : (s + 1) * size, base + size : base + 2 * size] = low
    span = pl.ds(2 * size * first, 2 * size * len(chosen))
    both = jnp.dot(stacked[...], weights_ref[span], preferred_element_type=F32)
    return both[:, :size] + both[:, size:]


def join_kernel(keep_ref, got_ref, packed_refs, out_ref):
    rows = keep_ref.shape[0]
    out_ref[:rows] = keep_ref[...] + got_ref[...]
    share = (out_ref.shape[0] - rows) // max(len(packed_refs), 1)
    for i, ref in enumerate(packed_refs):
        out_ref[rows + i * share : rows + (i + 1) * share] = ref[ref.shape[0] - share :]


def plane_kernel(part_refs, sum_ref, *diag_refs):
    rows = sum_ref.shape[0]
    size = rows - PAD
    summed = part_refs[0][:rows]
    for ref in part_refs[1:]:
        summed += ref[:rows]
    sum_ref[...] = summed
    chip = lax.axis_index("ops") // 2
    share = size // len(part_refs)
    for m, ref in enumerate(part_refs):
        first = pl.multiple_of(jnp.bitwise_xor(chip, m) * share, share)
        for i, diag_ref in enumerate(diag_refs):
            diag_ref[pl.ds(first, share)] = ref[rows + i * share : rows + (i + 1) * share]


def first_kernel(n_sec, n_ops, source_ref, coupling_ref, pairs_ref, weights_ref, local_ref, near_ref, mine_refs, theirs_refs,
                 keep_ref, send_ref, norm_ref, slots, stacked):
    size = local_ref.shape[1]
    core = lax.axis_index("ops") % 2
    acc = jnp.zeros((size, size), F32)
    for m in range(n_sec):
        for s in range(2):
            if m < 2:
                at, block = 2 * m + s, (local_ref[s], near_ref[s * size : (s + 1) * size])[m]
            else:
                at, block = 2 * m + (core if s == 0 else 1 - core), (mine_refs, theirs_refs)[s][m - 2][:size]
            acc += block * block
            store_vector(slots, at, block)
    slots[2 * n_sec] = jnp.zeros_like(slots[2 * n_sec])
    norm_ref[...] = jnp.broadcast_to(total(acc), norm_ref.shape)
    part = apply_terms(range(pairs_ref.shape[0]), n_sec, source_ref, pairs_ref, weights_ref, slots, stacked)
    corr = jnp.zeros((1, 1), F32)
    mirror = n_sec // 2
    blocks = []
    for s in range(2):
        if mirror < 2:
            partner = near_ref[s * size : (s + 1) * size]
        else:
            partner = jnp.where(core == s, mine_refs[mirror - 2][:size], theirs_refs[mirror - 2][:size])
        blocks.append(part[s * size : (s + 1) * size] + (coupling_ref[0, s] / n_ops) * partner.T)
        corr += total(local_ref[s] * blocks[s])
    keep_ref[:size] = jnp.where(core == 0, blocks[0], blocks[1])
    send_ref[:size] = jnp.where(core == 0, blocks[1], blocks[0])
    keep_ref[size:] = jnp.broadcast_to(corr, (PAD, size))
    send_ref[size:] = jnp.broadcast_to(corr, (PAD, size))


def correction_kernel(n_sec, norm_ref, whole_ref, near_ref, mine_refs, sum_refs, diag_refs, out_ref):
    size = whole_ref.shape[1]
    core = lax.axis_index("ops") % 2
    norm_sq = norm_ref[:1, :1]
    corr = sum_refs[0][size : size + 1, :1]
    for ref in sum_refs[1:]:
        corr += ref[size : size + 1, :1]
    scale = jnp.sqrt(norm_sq)
    inverse = 1.0 / scale
    rayleigh = corr / norm_sq
    sums = [jnp.zeros((size, size), F32) for _ in range(5)]
    for m in range(n_sec):
        if m < 2:
            ref = (whole_ref, near_ref)[m]
            wave = ref[pl.ds(pl.multiple_of(core * size, size), size)]
        else:
            wave = mine_refs[m - 2][:size]
        sigma = sum_refs[m][:size]
        resid = sigma * inverse - rayleigh * (wave * inverse)
        offset = diag_refs[m][...] - rayleigh
        corrected = resid / (1.0 + offset * offset)
        out_ref[m * size : (m + 1) * size] = corrected
        for i, factor in enumerate((wave, corrected, resid, sigma)):
            sums[i] += corrected * factor
        sums[4] += wave * resid
    out_ref[n_sec * size : (n_sec + 1) * size] = sum_refs[0][:size]
    tail = [spread(scale, size), spread(rayleigh, size)] + [spread(total(values), size) for values in sums]
    for i, row in enumerate(tail):
        out_ref[(n_sec + 1) * size + i : (n_sec + 1) * size + i + 1] = row
    for i in range(len(tail), PAD):
        out_ref[(n_sec + 1) * size + i : (n_sec + 1) * size + i + 1] = jnp.zeros((1, size), F32)


def rows_here(block, core):
    rows = block.shape[0] // 2
    return jnp.where(core == 0, block[:rows], block[rows:])


def even_kernel(n_sec, n_ops, source_ref, coupling_ref, pairs_ref, weights_ref, mine_ref, theirs_ref,
                slots, part_ref, curve_ref, own_ref, scalar_ref, stacked):
    size = pairs_ref.shape[2]
    core = lax.axis_index("ops") % 2
    for m in range(n_sec):
        span = pl.ds(m * size, size)
        store_vector(slots, 2 * m + core, mine_ref[span])
        store_vector(slots, 2 * m + 1 - core, theirs_ref[span])
    slots[2 * n_sec] = jnp.zeros_like(slots[2 * n_sec])
    part = apply_terms(range(0, pairs_ref.shape[0], 2), n_sec, source_ref, pairs_ref, weights_ref, slots, stacked)
    curve = jnp.zeros((1, 1), F32)
    mirror = pl.ds(n_sec // 2 * size, size)
    chip = lax.axis_index("ops") // 2
    share = 2 * own_ref.shape[1]
    for s in range(2):
        mine = core == s
        vec = jnp.where(mine, mine_ref[:size], theirs_ref[:size])
        partner = jnp.where(mine, mine_ref[mirror], theirs_ref[mirror])
        block = part[s * size : (s + 1) * size]
        mirrored = (coupling_ref[0, s] / n_ops) * partner.T
        part_ref[s] = block + mirrored
        for i, first in enumerate((0, n_sec)):
            span = pl.ds(pl.multiple_of(first * size + chip * share, share), share)
            own_ref[2 * i + s] = rows_here(jnp.where(mine, mine_ref[span], theirs_ref[span]), core)
        curve += total(vec * (2.0 * block + mirrored))
    curve_ref[...] = jnp.broadcast_to(curve, curve_ref.shape)
    tail = pl.ds((n_sec + 1) * size, PAD)
    row = lax.broadcasted_iota(jnp.int32, (PAD, size), 0)
    scalar_ref[...] = mine_ref[tail] + jnp.where(row < 2, 0.0, theirs_ref[tail])


def odd_kernel(n_sec, n_ops, source_ref, pairs_ref, weights_ref, slots, part_ref, keep_ref, send_ref, stacked):
    size = pairs_ref.shape[2]
    core = lax.axis_index("ops") % 2
    part = apply_terms(range(1, pairs_ref.shape[0], 2), n_sec, source_ref, pairs_ref, weights_ref, slots, stacked)
    rows = size // n_ops
    for s in range(2):
        block = part[s * size : (s + 1) * size] + part_ref[s]
        for q in range(n_ops // 2):
            at_row = (q * 2 + s) * rows
            even = block[2 * q * rows : (2 * q + 1) * rows]
            odd = block[(2 * q + 1) * rows : (2 * q + 2) * rows]
            keep_ref[at_row : at_row + rows] = jnp.where(core == 0, even, odd)
            send_ref[at_row : at_row + rows] = jnp.where(core == 0, odd, even)


def curve_kernel(keep_ref, send_ref, curve_refs, keep_out, send_out):
    size = keep_ref.shape[0]
    curve = curve_refs[0][...]
    for ref in curve_refs[1:]:
        curve += ref[...]
    for ref, out in ((keep_ref, keep_out), (send_ref, send_out)):
        out[:size] = ref[...]
        out[size:] = curve


def deal_kernel(keep_ref, got_ref, *out_refs):
    share = out_refs[0].shape[0] - PAD
    size = keep_ref.shape[0] - PAD
    chip = lax.axis_index("ops") // 2
    tail = keep_ref[size:] + got_ref[size:]
    for m, out_ref in enumerate(out_refs):
        span = pl.ds(pl.multiple_of(jnp.bitwise_xor(chip, m) * share, share), share)
        out_ref[:share] = keep_ref[span] + got_ref[span]
        out_ref[share:] = tail


def ritz_kernel(scalar_ref, local_ref, own_ref, got_refs, wave_out, sigma_out, energy_out):
    scale, rayleigh, wave_corr, corr_sq, corr_resid, corr_sigma, wave_resid = (scalar_ref[i : i + 1, :1] for i in range(7))
    rows = own_ref.shape[1]
    got = got_refs[0][...]
    for ref in got_refs[1:]:
        got += ref[...]
    curve = got[2 * rows : 2 * rows + 1, :1]
    ops = lax.axis_index("ops")
    core = ops % 2
    span = pl.ds(pl.multiple_of(ops // 2 * (2 * rows), 2 * rows), 2 * rows)
    along = wave_corr / scale
    lift = along / scale
    norm_sq = corr_sq - along * along
    norm = jnp.sqrt(norm_sq)
    coupling = (corr_resid - lift * wave_resid) / norm
    curvature = (curve - 2.0 * lift * corr_sigma + along * along * rayleigh) / norm_sq
    half_gap = 0.5 * (curvature - rayleigh)
    radius = jnp.sqrt(half_gap * half_gap + coupling * coupling)
    energy = 0.5 * (rayleigh + curvature) - radius
    safe = jnp.where(radius > 0.0, radius, 1.0)
    big = jnp.sqrt(0.5 + 0.5 * (jnp.abs(half_gap) / safe))
    small = (0.5 * (jnp.abs(coupling) / safe)) / big
    ahead = half_gap >= 0.0
    cos_part = jnp.where(radius > 0.0, jnp.where(ahead, big, small), 1.0)
    sin_size = jnp.where(radius > 0.0, jnp.where(ahead, small, big), 0.0)
    sin_part = jnp.where(coupling < 0.0, sin_size, -sin_size)
    factor = sin_part * scale / norm
    for s in range(2):
        wave, sigma = rows_here(local_ref[s, span], core), own_ref[2 + s]
        wave_out[s] = cos_part * wave + factor * (own_ref[s] - lift * wave)
        sigma_out[s] = cos_part * sigma + factor * (got[s * rows : (s + 1) * rows] - lift * sigma)
    energy_out[...] = jnp.broadcast_to(energy, energy_out.shape)


def body(n_ops, n_sec, wavefunction, hamiltonian_diag, mirror_coupling, left_env, right_env, term_source):
    owned, size, _ = wavefunction.shape
    terms = left_env.shape[0]
    half = terms // 4 * 2
    chips = n_ops // 2
    rows = size // n_ops
    shape = jax.ShapeDtypeStruct

    def swap(values):
        return lax.ppermute(values, "ops", [(i, i ^ 1) for i in range(n_ops)])

    def to_chip(values, m):
        return lax.ppermute(values, "ops", [(i, i ^ (2 * m)) for i in range(n_ops)])

    def to_plane(values, m):
        return lax.ppermute(values, "sec", [(i, i ^ m) for i in range(n_sec)])

    def gather_planes(values):
        return [values] + [to_plane(values, m) for m in range(1, n_sec)]

    matmul_flops = terms * owned * size * size * size * 12
    slot_shape = (2 * n_sec + 1, 2 * size, 2 * size)
    stack_shape = (owned * size, 2 * terms * size)
    half_shape = (owned * size, terms * size)
    message_shape = shape((size + PAD, size), F32)
    scalar_shape = shape((PAD, size), F32)

    def in_hbm(values):
        return pltpu.with_memory_space_constraint(values, pltpu.HBM)

    with jax.named_scope("gather_wave"):
        packed, whole, own_diag = call(
            pack_kernel,
            (
                shape((size + size // chips, size), F32),
                shape((owned * size + size // chips, size), F32),
                shape((size, size), F32),
            ),
            [HBM] * 2,
            [pltpu.SemaphoreType.DMA((owned + 4,))],
            limit=SMALL,
        )(in_hbm(wavefunction), in_hbm(hamiltonian_diag))
        mine = [to_plane(packed, m) for m in range(2, n_sec)]
        near = to_plane(whole, 1)
    with jax.named_scope("load"):
        held = [left_env, right_env, wavefunction, term_source.T, mirror_coupling[None]]
        loaded = call(
            load_kernel,
            (
                shape((terms, owned, size, 2 * size), BF16),
                shape((2 * terms * size, 2 * size), BF16),
                *(shape(values.shape, values.dtype) for values in held[2:]),
            ),
            [HBM] * len(held),
            [
                pltpu.VMEM(left_env.shape, F32),
                pltpu.VMEM(right_env.shape, F32),
                pltpu.SemaphoreType.DMA((len(held),)),
            ],
            limit=SMALL,
        )(*[in_hbm(values) for values in held])
        loaded, mine = lax.optimization_barrier((loaded, mine))
        pairs, weights, local, source, coupling = loaded
    with jax.named_scope("swap_wave"):
        theirs = [swap(values) for values in mine]
    with jax.named_scope("first_apply"):
        keep, send, norm = call(
            functools.partial(first_kernel, n_sec, n_ops),
            (message_shape, message_shape, scalar_shape),
            [SMEM, SMEM] + [VMEM] * 4 + [[VMEM] * (n_sec - 2)] * 2,
            [pltpu.VMEM(slot_shape, BF16), pltpu.VMEM(stack_shape, BF16)],
            matmul_flops,
        )(source, coupling, pairs, weights, local, near, mine, theirs)
    with jax.named_scope("reduce_sigma"):
        share = size // chips
        joined = call(
            join_kernel,
            shape((size + PAD + (n_sec - 1) * share, size), F32),
            [VMEM, VMEM, [VMEM] * (n_sec - 1)],
            limit=SMALL,
        )(keep, swap(send), [near] + mine)
        summed, *diag = call(
            plane_kernel,
            (message_shape, *[shape((size, size), F32)] * (n_sec - 1)),
            [[VMEM] * chips],
            limit=SMALL,
        )([joined] + [to_chip(joined, m) for m in range(1, chips)])
    with jax.named_scope("gather_sigma"):
        sums = gather_planes(summed)
    with jax.named_scope("correction"):
        found = call(
            functools.partial(correction_kernel, n_sec),
            shape(((n_sec + 1) * size + PAD, size), F32),
            [VMEM] * 3 + [[VMEM] * (n_sec - 2), [VMEM] * n_sec, [VMEM] * n_sec],
            limit=SMALL,
        )(norm, whole, near, mine, sums, [own_diag] + diag)
        other = swap(found)
    with jax.named_scope("even_terms"):
        slots, part, curve, kept, scalars = call(
            functools.partial(even_kernel, n_sec, n_ops),
            (
                shape(slot_shape, BF16),
                shape((owned, size, size), F32),
                scalar_shape,
                shape((2 * owned, rows, size), F32),
                scalar_shape,
            ),
            [SMEM, SMEM] + [VMEM] * 4,
            [pltpu.VMEM(half_shape, BF16)],
            matmul_flops // 2,
        )(source, coupling, pairs, weights, found, other)
        curves = gather_planes(curve)
    with jax.named_scope("odd_terms"):
        keep, send = call(
            functools.partial(odd_kernel, n_sec, n_ops),
            (shape((size, size), F32), shape((size, size), F32)),
            [SMEM] + [VMEM] * 4,
            [pltpu.VMEM(half_shape, BF16)],
            matmul_flops // 2,
        )(source, pairs, weights, slots, part)
    with jax.named_scope("reduce_dir_sigma"):
        keep, send = call(curve_kernel, (message_shape, message_shape), [VMEM, VMEM, [VMEM] * n_sec], limit=SMALL)(
            keep, send, curves
        )
        dealt = call(deal_kernel, [shape((2 * rows + PAD, size), F32)] * chips, [VMEM, VMEM], limit=SMALL)(keep, swap(send))
        got = [dealt[0]] + [to_chip(dealt[m], m) for m in range(1, chips)]
    with jax.named_scope("ritz"):
        new_wave, new_sigma, energy = call(
            ritz_kernel,
            (shape((owned, rows, size), F32), shape((owned, rows, size), F32), shape((1, size), F32)),
            [VMEM] * 3 + [[VMEM] * chips],
        )(scalars, local, kept, got)
    return (new_wave, new_sigma, energy[0, :1])


def solution(mesh):
    placed = (
        P("sec", None, None),
        P("sec", None, None),
        P("sec"),
        P("ops", "sec", None, None),
        P("ops", None, None),
        P("ops", "sec"),
    )
    return jax.shard_map(
        functools.partial(body, mesh.shape["ops"], mesh.shape["sec"]),
        mesh=mesh,
        in_specs=placed,
        out_specs=(P("sec", "ops", None), P("sec", "ops", None), P()),
        check_vma=False,
    )
```

```python
import functools

import jax
import jax.numpy as jnp
from jax import lax
from jax.experimental import pallas as pl
from jax.experimental.pallas import tpu as pltpu
from jax.sharding import PartitionSpec as P

F32 = jnp.float32
BF16 = jnp.bfloat16
VMEM = pl.BlockSpec(memory_space=pltpu.VMEM)
HBM = pl.BlockSpec(memory_space=pltpu.HBM)
SMEM = pl.BlockSpec(memory_space=pltpu.SMEM)
PAD = 8
LIMIT = 16 * 1024 * 1024
SMALL = 16 * 1024 * 1024


def call(kernel, out_shape, in_specs, scratch=(), flops=0, limit=LIMIT):
    return pl.pallas_call(
        kernel,
        out_shape=out_shape,
        in_specs=in_specs,
        out_specs=jax.tree.map(lambda _: VMEM, out_shape),
        scratch_shapes=list(scratch),
        compiler_params=pltpu.CompilerParams(vmem_limit_bytes=limit),
        cost_estimate=pl.CostEstimate(flops=flops, bytes_accessed=1 << 20, transcendentals=0),
    )


def split(values):
    high = values.astype(BF16)
    return high, (values - high.astype(F32)).astype(BF16)


def total(values):
    return jnp.sum(values, keepdims=True)


def spread(value, size):
    return jnp.broadcast_to(value, (1, size))


def position(k, terms):
    return k // 2 + k % 2 * (terms // 2)


def load_kernel(left_ref, right_ref, wave_ref, source_ref, coupling_ref,
                pairs_ref, weights_ref, local_ref, sources_ref, couplings_ref, left_buf, right_buf, sems):
    terms, owned, size, _ = left_ref.shape
    sources = (left_ref, right_ref, wave_ref, source_ref, coupling_ref)
    targets = (left_buf, right_buf, local_ref, sources_ref, couplings_ref)
    copies = [pltpu.make_async_copy(source, target, sems.at[i]) for i, (source, target) in enumerate(zip(sources, targets))]
    for copy in copies:
        copy.start()
    for copy in copies:
        copy.wait()
    for k in range(terms):
        for s in range(owned):
            pairs_ref[k, s, :, :size], pairs_ref[k, s, :, size:] = split(left_buf[k, s])
        base = 2 * size * position(k, terms)
        high, low = split(right_buf[k ^ 1])
        weights_ref[base : base + size, :size] = high
        weights_ref[base : base + size, size:] = low
        weights_ref[base + size : base + 2 * size, :size] = high
        weights_ref[base + size : base + 2 * size, size:] = jnp.zeros_like(high)


def pack_kernel(wave_ref, diag_ref, packed_ref, own_diag_ref, sems):
    size = wave_ref.shape[1]
    share = packed_ref.shape[0] - size
    ops = lax.axis_index("ops")
    core, chip = ops % 2, ops // 2
    rows = pl.ds(pl.multiple_of(chip * share, share), share)
    moves = [
        (wave_ref.at[core], packed_ref.at[pl.ds(0, size)]),
        (diag_ref.at[core, rows], packed_ref.at[pl.ds(size, share)]),
        (diag_ref.at[core], own_diag_ref),
    ]
    copies = [pltpu.make_async_copy(source, target, sems.at[i]) for i, (source, target) in enumerate(moves)]
    for copy in copies:
        copy.start()
    for copy in copies:
        copy.wait()


def other_kernel(source_ref, target_ref):
    target_ref[...] = source_ref[1 - lax.axis_index("ops") % 2]


def partners(n_sec):
    return [(m, m + 1) for m in range(1, n_sec - 1, 2)], n_sec - 1


def from_partner(n_sec, m, core, mine, theirs, last):
    for i, pair in enumerate(partners(n_sec)[0]):
        if m in pair:
            return jnp.where(core == pair.index(m), mine(i), theirs(i))
    return last()


def store_vector(slots, at, block):
    size = block.shape[0]
    high, low = split(block)
    slots[at, :size, :size] = high
    slots[at, :size, size:] = low
    slots[at, size:, :size] = high
    slots[at, size:, size:] = jnp.zeros_like(high)


def apply_terms(chosen, n_sec, source_ref, pairs_ref, weights_ref, slots, stacked):
    terms, owned, size, _ = pairs_ref.shape
    plane = lax.axis_index("sec")
    first = position(chosen[0], terms)
    for k in chosen:
        base = 2 * size * (position(k, terms) - first)
        for s in range(owned):
            source = source_ref[s, k]
            at = 2 * jnp.bitwise_xor(source // 2, plane) + jnp.bitwise_and(source, 1)
            inner = jnp.dot(pairs_ref[k, s], slots[jnp.where(source < 0, 2 * n_sec, at)], preferred_element_type=F32)
            high, low = split(inner[:, :size] + inner[:, size:])
            stacked[s * size : (s + 1) * size, base : base + size] = high
            stacked[s * size : (s + 1) * size, base + size : base + 2 * size] = low
    span = pl.ds(2 * size * first, 2 * size * len(chosen))
    both = jnp.dot(stacked[...], weights_ref[span], preferred_element_type=F32)
    return both[:, :size] + both[:, size:]


def join_kernel(keep_ref, got_ref, last_ref, out_ref):
    rows, size = keep_ref.shape
    out_ref[:rows] = keep_ref[...] + got_ref[...]
    out_ref[rows:] = last_ref[size:]


def plane_kernel(part_refs, sum_ref, diag_ref):
    rows = sum_ref.shape[0]
    summed = part_refs[0][:rows]
    for ref in part_refs[1:]:
        summed += ref[:rows]
    sum_ref[...] = summed
    chip = lax.axis_index("ops") // 2
    share = diag_ref.shape[0] // len(part_refs)
    for m, ref in enumerate(part_refs):
        first = pl.multiple_of(jnp.bitwise_xor(chip, m) * share, share)
        diag_ref[pl.ds(first, share)] = ref[rows:]


def first_kernel(n_sec, n_ops, source_ref, coupling_ref, pairs_ref, weights_ref, local_ref, mine_refs, theirs_refs,
                 last_ref, other_last_ref, keep_ref, send_ref, norm_ref, slots, stacked):
    size = local_ref.shape[1]
    core = lax.axis_index("ops") % 2
    pairs, last = partners(n_sec)
    blocks = [(s, local_ref[s]) for s in range(2)]
    for i, (even, odd) in enumerate(pairs):
        for refs, m in ((mine_refs, jnp.where(core == 0, even, odd)), (theirs_refs, jnp.where(core == 0, odd, even))):
            blocks += [(2 * m + s, refs[i][s]) for s in range(2)]
    blocks += [(2 * last + core, last_ref[:size]), (2 * last + 1 - core, other_last_ref[:size])]
    acc = jnp.zeros((size, size), F32)
    for at, block in blocks:
        acc += block * block
        store_vector(slots, at, block)
    slots[2 * n_sec] = jnp.zeros_like(slots[2 * n_sec])
    norm_ref[...] = jnp.broadcast_to(total(acc), norm_ref.shape)
    part = apply_terms(range(pairs_ref.shape[0]), n_sec, source_ref, pairs_ref, weights_ref, slots, stacked)
    corr = jnp.zeros((1, 1), F32)
    blocks = []
    for s in range(2):
        partner = from_partner(
            n_sec, n_sec // 2, core, lambda i: mine_refs[i][s], lambda i: theirs_refs[i][s],
            lambda: jnp.where(core == s, last_ref[:size], other_last_ref[:size]),
        )
        blocks.append(part[s * size : (s + 1) * size] + (coupling_ref[0, s] / n_ops) * partner.T)
        corr += total(local_ref[s] * blocks[s])
    keep_ref[:size] = jnp.where(core == 0, blocks[0], blocks[1])
    send_ref[:size] = jnp.where(core == 0, blocks[1], blocks[0])
    keep_ref[size:] = jnp.broadcast_to(corr, (PAD, size))
    send_ref[size:] = jnp.broadcast_to(corr, (PAD, size))


def correction_kernel(n_sec, norm_ref, sector_refs, mine_refs, theirs_refs, last_refs, diag_refs, other_diag_refs, sum_refs, out_ref):
    size = sector_refs[1].shape[0]
    core = lax.axis_index("ops") % 2
    norm_sq = norm_ref[:1, :1]
    corr = sum_refs[0][size : size + 1, :1]
    for ref in sum_refs[1:]:
        corr += ref[size : size + 1, :1]
    scale = jnp.sqrt(norm_sq)
    inverse = 1.0 / scale
    rayleigh = corr / norm_sq
    sums = [jnp.zeros((size, size), F32) for _ in range(5)]
    for m in range(n_sec):
        if m == 0:
            wave, diag = sector_refs[0][:size], sector_refs[1][...]
        else:
            wave = from_partner(
                n_sec, m, core, lambda i: mine_refs[i][core], lambda i: theirs_refs[i][core], lambda: last_refs[0][:size]
            )
            diag = from_partner(
                n_sec, m, core, lambda i: diag_refs[i][core], lambda i: other_diag_refs[i][...], lambda: last_refs[1][...]
            )
        sigma = sum_refs[m][:size]
        resid = sigma * inverse - rayleigh * (wave * inverse)
        offset = diag - rayleigh
        corrected = resid / (1.0 + offset * offset)
        out_ref[m * size : (m + 1) * size] = corrected
        for i, factor in enumerate((wave, corrected, resid, sigma)):
            sums[i] += corrected * factor
        sums[4] += wave * resid
    out_ref[n_sec * size : (n_sec + 1) * size] = sum_refs[0][:size]
    tail = [spread(scale, size), spread(rayleigh, size)] + [spread(total(values), size) for values in sums]
    for i, row in enumerate(tail):
        out_ref[(n_sec + 1) * size + i : (n_sec + 1) * size + i + 1] = row
    for i in range(len(tail), PAD):
        out_ref[(n_sec + 1) * size + i : (n_sec + 1) * size + i + 1] = jnp.zeros((1, size), F32)


def rows_here(block, core):
    rows = block.shape[0] // 2
    return jnp.where(core == 0, block[:rows], block[rows:])


def even_kernel(n_sec, n_ops, source_ref, coupling_ref, pairs_ref, weights_ref, mine_ref, theirs_ref,
                slots, part_ref, curve_ref, own_ref, scalar_ref, stacked):
    size = pairs_ref.shape[2]
    core = lax.axis_index("ops") % 2
    for m in range(n_sec):
        span = pl.ds(m * size, size)
        store_vector(slots, 2 * m + core, mine_ref[span])
        store_vector(slots, 2 * m + 1 - core, theirs_ref[span])
    slots[2 * n_sec] = jnp.zeros_like(slots[2 * n_sec])
    part = apply_terms(range(0, pairs_ref.shape[0], 2), n_sec, source_ref, pairs_ref, weights_ref, slots, stacked)
    curve = jnp.zeros((1, 1), F32)
    mirror = pl.ds(n_sec // 2 * size, size)
    chip = lax.axis_index("ops") // 2
    share = 2 * own_ref.shape[1]
    for s in range(2):
        mine = core == s
        vec = jnp.where(mine, mine_ref[:size], theirs_ref[:size])
        partner = jnp.where(mine, mine_ref[mirror], theirs_ref[mirror])
        block = part[s * size : (s + 1) * size]
        mirrored = (coupling_ref[0, s] / n_ops) * partner.T
        part_ref[s] = block + mirrored
        for i, first in enumerate((0, n_sec)):
            span = pl.ds(pl.multiple_of(first * size + chip * share, share), share)
            own_ref[2 * i + s] = rows_here(jnp.where(mine, mine_ref[span], theirs_ref[span]), core)
        curve += total(vec * (2.0 * block + mirrored))
    curve_ref[...] = jnp.broadcast_to(curve, curve_ref.shape)
    tail = pl.ds((n_sec + 1) * size, PAD)
    row = lax.broadcasted_iota(jnp.int32, (PAD, size), 0)
    scalar_ref[...] = mine_ref[tail] + jnp.where(row < 2, 0.0, theirs_ref[tail])


def odd_kernel(n_sec, n_ops, source_ref, pairs_ref, weights_ref, slots, part_ref, keep_ref, send_ref, stacked):
    size = pairs_ref.shape[2]
    core = lax.axis_index("ops") % 2
    part = apply_terms(range(1, pairs_ref.shape[0], 2), n_sec, source_ref, pairs_ref, weights_ref, slots, stacked)
    rows = size // n_ops
    for s in range(2):
        block = part[s * size : (s + 1) * size] + part_ref[s]
        for q in range(n_ops // 2):
            at_row = (q * 2 + s) * rows
            even = block[2 * q * rows : (2 * q + 1) * rows]
            odd = block[(2 * q + 1) * rows : (2 * q + 2) * rows]
            keep_ref[at_row : at_row + rows] = jnp.where(core == 0, even, odd)
            send_ref[at_row : at_row + rows] = jnp.where(core == 0, odd, even)


def curve_kernel(keep_ref, send_ref, curve_refs, keep_out, send_out):
    size = keep_ref.shape[0]
    curve = curve_refs[0][...]
    for ref in curve_refs[1:]:
        curve += ref[...]
    for ref, out in ((keep_ref, keep_out), (send_ref, send_out)):
        out[:size] = ref[...]
        out[size:] = curve


def deal_kernel(keep_ref, got_ref, *out_refs):
    share = out_refs[0].shape[0] - PAD
    size = keep_ref.shape[0] - PAD
    chip = lax.axis_index("ops") // 2
    tail = keep_ref[size:] + got_ref[size:]
    for m, out_ref in enumerate(out_refs):
        span = pl.ds(pl.multiple_of(jnp.bitwise_xor(chip, m) * share, share), share)
        out_ref[:share] = keep_ref[span] + got_ref[span]
        out_ref[share:] = tail


def ritz_kernel(scalar_ref, local_ref, own_ref, got_refs, wave_out, sigma_out, energy_out):
    scale, rayleigh, wave_corr, corr_sq, corr_resid, corr_sigma, wave_resid = (scalar_ref[i : i + 1, :1] for i in range(7))
    rows = own_ref.shape[1]
    got = got_refs[0][...]
    for ref in got_refs[1:]:
        got += ref[...]
    curve = got[2 * rows : 2 * rows + 1, :1]
    ops = lax.axis_index("ops")
    core = ops % 2
    span = pl.ds(pl.multiple_of(ops // 2 * (2 * rows), 2 * rows), 2 * rows)
    along = wave_corr / scale
    lift = along / scale
    norm_sq = corr_sq - along * along
    norm = jnp.sqrt(norm_sq)
    coupling = (corr_resid - lift * wave_resid) / norm
    curvature = (curve - 2.0 * lift * corr_sigma + along * along * rayleigh) / norm_sq
    half_gap = 0.5 * (curvature - rayleigh)
    radius = jnp.sqrt(half_gap * half_gap + coupling * coupling)
    energy = 0.5 * (rayleigh + curvature) - radius
    safe = jnp.where(radius > 0.0, radius, 1.0)
    big = jnp.sqrt(0.5 + 0.5 * (jnp.abs(half_gap) / safe))
    small = (0.5 * (jnp.abs(coupling) / safe)) / big
    ahead = half_gap >= 0.0
    cos_part = jnp.where(radius > 0.0, jnp.where(ahead, big, small), 1.0)
    sin_size = jnp.where(radius > 0.0, jnp.where(ahead, small, big), 0.0)
    sin_part = jnp.where(coupling < 0.0, sin_size, -sin_size)
    factor = sin_part * scale / norm
    for s in range(2):
        wave, sigma = rows_here(local_ref[s, span], core), own_ref[2 + s]
        wave_out[s] = cos_part * wave + factor * (own_ref[s] - lift * wave)
        sigma_out[s] = cos_part * sigma + factor * (got[s * rows : (s + 1) * rows] - lift * sigma)
    energy_out[...] = jnp.broadcast_to(energy, energy_out.shape)


def body(n_ops, n_sec, wavefunction, hamiltonian_diag, mirror_coupling, left_env, right_env, term_source):
    owned, size, _ = wavefunction.shape
    terms = left_env.shape[0]
    half = terms // 4 * 2
    chips = n_ops // 2
    rows = size // n_ops
    shape = jax.ShapeDtypeStruct

    def swap(values):
        return lax.ppermute(values, "ops", [(i, i ^ 1) for i in range(n_ops)])

    def to_chip(values, m):
        return lax.ppermute(values, "ops", [(i, i ^ (2 * m)) for i in range(n_ops)])

    def to_plane(values, m):
        return lax.ppermute(values, "sec", [(i, i ^ m) for i in range(n_sec)])

    def to_planes(values, pair):
        moves = [(o * n_sec + z, o * n_sec + (z ^ pair[o % 2])) for o in range(n_ops) for z in range(n_sec)]
        return lax.ppermute(values, ("ops", "sec"), moves)

    def gather_planes(values):
        return [values] + [to_plane(values, m) for m in range(1, n_sec)]

    matmul_flops = terms * owned * size * size * size * 12
    slot_shape = (2 * n_sec + 1, 2 * size, 2 * size)
    stack_shape = (owned * size, 2 * terms * size)
    half_shape = (owned * size, terms * size)
    message_shape = shape((size + PAD, size), F32)
    scalar_shape = shape((PAD, size), F32)

    def in_hbm(values):
        return pltpu.with_memory_space_constraint(values, pltpu.HBM)

    zs, last = partners(n_sec)

    with jax.named_scope("gather_wave"):
        mine = [to_planes(wavefunction, pair) for pair in zs]
        sectors = call(
            pack_kernel,
            (shape((size + size // chips, size), F32), shape((size, size), F32)),
            [HBM] * 2,
            [pltpu.SemaphoreType.DMA((3,))],
            limit=SMALL,
        )(in_hbm(wavefunction), in_hbm(hamiltonian_diag))
        mine.append(to_plane(sectors[0], last))
    with jax.named_scope("gather_diag"):
        diag = [to_planes(hamiltonian_diag, pair) for pair in zs]
    with jax.named_scope("load"):
        held = [left_env, right_env, wavefunction, term_source.T, mirror_coupling[None]]
        loaded = call(
            load_kernel,
            (
                shape((terms, owned, size, 2 * size), BF16),
                shape((2 * terms * size, 2 * size), BF16),
                *(shape(values.shape, values.dtype) for values in held[2:]),
            ),
            [HBM] * len(held),
            [
                pltpu.VMEM(left_env.shape, F32),
                pltpu.VMEM(right_env.shape, F32),
                pltpu.SemaphoreType.DMA((len(held),)),
            ],
            limit=SMALL,
        )(*[in_hbm(values) for values in held])
        loaded, mine = lax.optimization_barrier((loaded, mine))
        pairs, weights, local, source, coupling = loaded
    with jax.named_scope("swap_wave"):
        theirs = [swap(values) for values in mine]
        (*mine, last), (*theirs, other_last) = mine, theirs
    with jax.named_scope("first_apply"):
        keep, send, norm = call(
            functools.partial(first_kernel, n_sec, n_ops),
            (message_shape, message_shape, scalar_shape),
            [SMEM, SMEM] + [VMEM] * 3 + [[VMEM] * len(zs)] * 2 + [VMEM] * 2,
            [pltpu.VMEM(slot_shape, BF16), pltpu.VMEM(stack_shape, BF16)],
            matmul_flops,
        )(source, coupling, pairs, weights, local, mine, theirs, last, other_last)
    with jax.named_scope("reduce_sigma"):
        joined = call(
            join_kernel, shape((size + PAD + size // chips, size), F32), [VMEM] * 3, limit=SMALL
        )(keep, swap(send), last)
        summed, last_diag = call(
            plane_kernel, (message_shape, shape((size, size), F32)), [[VMEM] * chips], limit=SMALL
        )([joined] + [to_chip(joined, m) for m in range(1, chips)])
    with jax.named_scope("swap_diag"):
        other_diag = [
            swap(call(other_kernel, shape((size, size), F32), [VMEM], limit=SMALL)(values)) for values in diag
        ]
    with jax.named_scope("gather_sigma"):
        sums = gather_planes(summed)
    with jax.named_scope("correction"):
        found = call(
            functools.partial(correction_kernel, n_sec),
            shape(((n_sec + 1) * size + PAD, size), F32),
            [VMEM, [VMEM] * 2, [VMEM] * len(zs), [VMEM] * len(zs), [VMEM] * 2, [VMEM] * len(zs), [VMEM] * len(zs), [VMEM] * n_sec],
            limit=SMALL,
        )(norm, list(sectors), mine, theirs, [last, last_diag], diag, other_diag, sums)
        other = swap(found)
    with jax.named_scope("even_terms"):
        slots, part, curve, kept, scalars = call(
            functools.partial(even_kernel, n_sec, n_ops),
            (
                shape(slot_shape, BF16),
                shape((owned, size, size), F32),
                scalar_shape,
                shape((2 * owned, rows, size), F32),
                scalar_shape,
            ),
            [SMEM, SMEM] + [VMEM] * 4,
            [pltpu.VMEM(half_shape, BF16)],
            matmul_flops // 2,
        )(source, coupling, pairs, weights, found, other)
        curves = gather_planes(curve)
    with jax.named_scope("odd_terms"):
        keep, send = call(
            functools.partial(odd_kernel, n_sec, n_ops),
            (shape((size, size), F32), shape((size, size), F32)),
            [SMEM] + [VMEM] * 4,
            [pltpu.VMEM(half_shape, BF16)],
            matmul_flops // 2,
        )(source, pairs, weights, slots, part)
    with jax.named_scope("reduce_dir_sigma"):
        keep, send = call(curve_kernel, (message_shape, message_shape), [VMEM, VMEM, [VMEM] * n_sec], limit=SMALL)(
            keep, send, curves
        )
        dealt = call(deal_kernel, [shape((2 * rows + PAD, size), F32)] * chips, [VMEM, VMEM], limit=SMALL)(keep, swap(send))
        got = [dealt[0]] + [to_chip(dealt[m], m) for m in range(1, chips)]
    with jax.named_scope("ritz"):
        new_wave, new_sigma, energy = call(
            ritz_kernel,
            (shape((owned, rows, size), F32), shape((owned, rows, size), F32), shape((1, size), F32)),
            [VMEM] * 3 + [[VMEM] * chips],
        )(scalars, local, kept, got)
    return (new_wave, new_sigma, energy[0, :1])


def solution(mesh):
    placed = (
        P("sec", None, None),
        P("sec", None, None),
        P("sec"),
        P("ops", "sec", None, None),
        P("ops", None, None),
        P("ops", "sec"),
    )
    return jax.shard_map(
        functools.partial(body, mesh.shape["ops"], mesh.shape["sec"]),
        mesh=mesh,
        in_specs=placed,
        out_specs=(P("sec", "ops", None), P("sec", "ops", None), P()),
        check_vma=False,
    )
```

```python
import functools

import jax
import jax.numpy as jnp
from jax import lax
from jax.experimental import pallas as pl
from jax.experimental.pallas import tpu as pltpu
from jax.sharding import PartitionSpec as P

F32 = jnp.float32
BF16 = jnp.bfloat16
VMEM = pl.BlockSpec(memory_space=pltpu.VMEM)
HBM = pl.BlockSpec(memory_space=pltpu.HBM)
SMEM = pl.BlockSpec(memory_space=pltpu.SMEM)
PAD = 8
LIMIT = 16 * 1024 * 1024
SMALL = 16 * 1024 * 1024


def call(kernel, out_shape, in_specs, scratch=(), flops=0, limit=LIMIT):
    return pl.pallas_call(
        kernel,
        out_shape=out_shape,
        in_specs=in_specs,
        out_specs=jax.tree.map(lambda _: VMEM, out_shape),
        scratch_shapes=list(scratch),
        compiler_params=pltpu.CompilerParams(vmem_limit_bytes=limit),
        cost_estimate=pl.CostEstimate(flops=flops, bytes_accessed=1 << 20, transcendentals=0),
    )


def split(values):
    high = values.astype(BF16)
    return high, (values - high.astype(F32)).astype(BF16)


def total(values):
    return jnp.sum(values, keepdims=True)


def spread(value, size):
    return jnp.broadcast_to(value, (1, size))


def position(k, terms):
    return k // 2 + k % 2 * (terms // 2)


def load_kernel(left_ref, right_ref, wave_ref, source_ref, coupling_ref,
                pairs_ref, weights_ref, local_ref, sources_ref, couplings_ref, left_buf, right_buf, sems):
    terms, owned, size, _ = left_ref.shape
    sources = (left_ref, right_ref, wave_ref, source_ref, coupling_ref)
    targets = (left_buf, right_buf, local_ref, sources_ref, couplings_ref)
    copies = [pltpu.make_async_copy(source, target, sems.at[i]) for i, (source, target) in enumerate(zip(sources, targets))]
    for copy in copies:
        copy.start()
    for copy in copies:
        copy.wait()
    for k in range(terms):
        for s in range(owned):
            pairs_ref[k, s, :, :size], pairs_ref[k, s, :, size:] = split(left_buf[k, s])
        base = 2 * size * position(k, terms)
        high, low = split(right_buf[k ^ 1])
        weights_ref[base : base + size, :size] = high
        weights_ref[base : base + size, size:] = low
        weights_ref[base + size : base + 2 * size, :size] = high
        weights_ref[base + size : base + 2 * size, size:] = jnp.zeros_like(high)


def pack_kernel(wave_ref, diag_ref, packed_ref, own_diag_ref, sems):
    size = wave_ref.shape[1]
    share = packed_ref.shape[0] - size
    ops = lax.axis_index("ops")
    core, chip = ops % 2, ops // 2
    rows = pl.ds(pl.multiple_of(chip * share, share), share)
    moves = [
        (wave_ref.at[core], packed_ref.at[pl.ds(0, size)]),
        (diag_ref.at[core, rows], packed_ref.at[pl.ds(size, share)]),
        (diag_ref.at[core], own_diag_ref),
    ]
    copies = [pltpu.make_async_copy(source, target, sems.at[i]) for i, (source, target) in enumerate(moves)]
    for copy in copies:
        copy.start()
    for copy in copies:
        copy.wait()


def other_kernel(source_ref, target_ref):
    target_ref[...] = source_ref[1 - lax.axis_index("ops") % 2]


def partners(n_sec):
    return [(m, m + 1) for m in range(1, n_sec - 1, 2)], n_sec - 1


def from_partner(n_sec, m, core, mine, theirs, last):
    for i, pair in enumerate(partners(n_sec)[0]):
        if m in pair:
            return jnp.where(core == pair.index(m), mine(i), theirs(i))
    return last()


def store_vector(slots, at, block):
    size = block.shape[0]
    high, low = split(block)
    slots[at, :size, :size] = high
    slots[at, :size, size:] = low
    slots[at, size:, :size] = high
    slots[at, size:, size:] = jnp.zeros_like(high)


def apply_terms(chosen, n_sec, source_ref, pairs_ref, weights_ref, slots, stacked):
    terms, owned, size, _ = pairs_ref.shape
    plane = lax.axis_index("sec")
    first = position(chosen[0], terms)
    for k in chosen:
        base = 2 * size * (position(k, terms) - first)
        for s in range(owned):
            source = source_ref[s, k]
            at = 2 * jnp.bitwise_xor(source // 2, plane) + jnp.bitwise_and(source, 1)
            inner = jnp.dot(pairs_ref[k, s], slots[jnp.where(source < 0, 2 * n_sec, at)], preferred_element_type=F32)
            high, low = split(inner[:, :size] + inner[:, size:])
            stacked[s * size : (s + 1) * size, base : base + size] = high
            stacked[s * size : (s + 1) * size, base + size : base + 2 * size] = low
    span = pl.ds(2 * size * first, 2 * size * len(chosen))
    both = jnp.dot(stacked[...], weights_ref[span], preferred_element_type=F32)
    return both[:, :size] + both[:, size:]


def join_kernel(keep_ref, got_ref, last_ref, out_ref):
    rows, size = keep_ref.shape
    out_ref[:rows] = keep_ref[...] + got_ref[...]
    out_ref[rows:] = last_ref[size:]


def plane_kernel(part_refs, sum_ref, diag_ref):
    rows = sum_ref.shape[0]
    summed = part_refs[0][:rows]
    for ref in part_refs[1:]:
        summed += ref[:rows]
    sum_ref[...] = summed
    chip = lax.axis_index("ops") // 2
    share = diag_ref.shape[0] // len(part_refs)
    for m, ref in enumerate(part_refs):
        first = pl.multiple_of(jnp.bitwise_xor(chip, m) * share, share)
        diag_ref[pl.ds(first, share)] = ref[rows:]


def first_kernel(n_sec, n_ops, source_ref, coupling_ref, pairs_ref, weights_ref, local_ref, mine_refs, theirs_refs,
                 last_ref, other_last_ref, keep_ref, send_ref, norm_ref, slots, stacked):
    size = local_ref.shape[1]
    core = lax.axis_index("ops") % 2
    pairs, last = partners(n_sec)
    blocks = [(s, local_ref[s]) for s in range(2)]
    for i, (even, odd) in enumerate(pairs):
        for refs, m in ((mine_refs, jnp.where(core == 0, even, odd)), (theirs_refs, jnp.where(core == 0, odd, even))):
            blocks += [(2 * m + s, refs[i][s]) for s in range(2)]
    blocks += [(2 * last + core, last_ref[:size]), (2 * last + 1 - core, other_last_ref[:size])]
    acc = jnp.zeros((size, size), F32)
    for at, block in blocks:
        acc += block * block
        store_vector(slots, at, block)
    slots[2 * n_sec] = jnp.zeros_like(slots[2 * n_sec])
    norm_ref[...] = jnp.broadcast_to(total(acc), norm_ref.shape)
    part = apply_terms(range(pairs_ref.shape[0]), n_sec, source_ref, pairs_ref, weights_ref, slots, stacked)
    corr = jnp.zeros((1, 1), F32)
    blocks = []
    for s in range(2):
        partner = from_partner(
            n_sec, n_sec // 2, core, lambda i: mine_refs[i][s], lambda i: theirs_refs[i][s],
            lambda: jnp.where(core == s, last_ref[:size], other_last_ref[:size]),
        )
        blocks.append(part[s * size : (s + 1) * size] + (coupling_ref[:, s : s + 1] * (1.0 / n_ops)) * partner.T)
        corr += total(local_ref[s] * blocks[s])
    keep_ref[:size] = jnp.where(core == 0, blocks[0], blocks[1])
    send_ref[:size] = jnp.where(core == 0, blocks[1], blocks[0])
    keep_ref[size:] = jnp.broadcast_to(corr, (PAD, size))
    send_ref[size:] = jnp.broadcast_to(corr, (PAD, size))


def correction_kernel(n_sec, norm_ref, sector_refs, mine_refs, theirs_refs, last_refs, diag_refs, other_diag_refs, sum_refs, out_ref):
    size = sector_refs[1].shape[0]
    core = lax.axis_index("ops") % 2
    norm_sq = norm_ref[:1, :1]
    corr = sum_refs[0][size : size + 1, :1]
    for ref in sum_refs[1:]:
        corr += ref[size : size + 1, :1]
    scale = jnp.sqrt(norm_sq)
    inverse = 1.0 / scale
    rayleigh = corr / norm_sq
    sums = [jnp.zeros((size, size), F32) for _ in range(5)]
    for m in range(n_sec):
        if m == 0:
            wave, diag = sector_refs[0][:size], sector_refs[1][...]
        else:
            wave = from_partner(
                n_sec, m, core, lambda i: mine_refs[i][core], lambda i: theirs_refs[i][core], lambda: last_refs[0][:size]
            )
            diag = from_partner(
                n_sec, m, core, lambda i: diag_refs[i][core], lambda i: other_diag_refs[i][...], lambda: last_refs[1][...]
            )
        sigma = sum_refs[m][:size]
        resid = sigma * inverse - rayleigh * (wave * inverse)
        offset = diag - rayleigh
        corrected = resid / (1.0 + offset * offset)
        out_ref[m * size : (m + 1) * size] = corrected
        for i, factor in enumerate((wave, corrected, resid, sigma)):
            sums[i] += corrected * factor
        sums[4] += wave * resid
    out_ref[n_sec * size : (n_sec + 1) * size] = sum_refs[0][:size]
    tail = [spread(scale, size), spread(rayleigh, size)] + [spread(total(values), size) for values in sums]
    for i, row in enumerate(tail):
        out_ref[(n_sec + 1) * size + i : (n_sec + 1) * size + i + 1] = row
    for i in range(len(tail), PAD):
        out_ref[(n_sec + 1) * size + i : (n_sec + 1) * size + i + 1] = jnp.zeros((1, size), F32)


def rows_here(block, core):
    rows = block.shape[0] // 2
    return jnp.where(core == 0, block[:rows], block[rows:])


def even_kernel(n_sec, n_ops, source_ref, coupling_ref, pairs_ref, weights_ref, mine_ref, theirs_ref,
                slots, part_ref, curve_ref, own_ref, scalar_ref, stacked):
    size = pairs_ref.shape[2]
    core = lax.axis_index("ops") % 2
    for m in range(n_sec):
        span = pl.ds(m * size, size)
        store_vector(slots, 2 * m + core, mine_ref[span])
        store_vector(slots, 2 * m + 1 - core, theirs_ref[span])
    slots[2 * n_sec] = jnp.zeros_like(slots[2 * n_sec])
    part = apply_terms(range(0, pairs_ref.shape[0], 2), n_sec, source_ref, pairs_ref, weights_ref, slots, stacked)
    curve = jnp.zeros((1, 1), F32)
    mirror = pl.ds(n_sec // 2 * size, size)
    chip = lax.axis_index("ops") // 2
    share = 2 * own_ref.shape[1]
    for s in range(2):
        mine = core == s
        vec = jnp.where(mine, mine_ref[:size], theirs_ref[:size])
        partner = jnp.where(mine, mine_ref[mirror], theirs_ref[mirror])
        block = part[s * size : (s + 1) * size]
        mirrored = (coupling_ref[:, s : s + 1] * (1.0 / n_ops)) * partner.T
        part_ref[s] = block + mirrored
        for i, first in enumerate((0, n_sec)):
            span = pl.ds(pl.multiple_of(first * size + chip * share, share), share)
            own_ref[2 * i + s] = rows_here(jnp.where(mine, mine_ref[span], theirs_ref[span]), core)
        curve += total(vec * (2.0 * block + mirrored))
    curve_ref[...] = jnp.broadcast_to(curve, curve_ref.shape)
    tail = pl.ds((n_sec + 1) * size, PAD)
    row = lax.broadcasted_iota(jnp.int32, (PAD, size), 0)
    scalar_ref[...] = mine_ref[tail] + jnp.where(row < 2, 0.0, theirs_ref[tail])


def odd_kernel(n_sec, n_ops, source_ref, pairs_ref, weights_ref, slots, part_ref, keep_ref, send_ref, stacked):
    size = pairs_ref.shape[2]
    core = lax.axis_index("ops") % 2
    part = apply_terms(range(1, pairs_ref.shape[0], 2), n_sec, source_ref, pairs_ref, weights_ref, slots, stacked)
    rows = size // n_ops
    for s in range(2):
        block = part[s * size : (s + 1) * size] + part_ref[s]
        for q in range(n_ops // 2):
            at_row = (q * 2 + s) * rows
            even = block[2 * q * rows : (2 * q + 1) * rows]
            odd = block[(2 * q + 1) * rows : (2 * q + 2) * rows]
            keep_ref[at_row : at_row + rows] = jnp.where(core == 0, even, odd)
            send_ref[at_row : at_row + rows] = jnp.where(core == 0, odd, even)


def curve_kernel(keep_ref, send_ref, curve_refs, keep_out, send_out):
    size = keep_ref.shape[0]
    curve = curve_refs[0][...]
    for ref in curve_refs[1:]:
        curve += ref[...]
    for ref, out in ((keep_ref, keep_out), (send_ref, send_out)):
        out[:size] = ref[...]
        out[size:] = curve


def deal_kernel(keep_ref, got_ref, *out_refs):
    share = out_refs[0].shape[0] - PAD
    size = keep_ref.shape[0] - PAD
    chip = lax.axis_index("ops") // 2
    tail = keep_ref[size:] + got_ref[size:]
    for m, out_ref in enumerate(out_refs):
        span = pl.ds(pl.multiple_of(jnp.bitwise_xor(chip, m) * share, share), share)
        out_ref[:share] = keep_ref[span] + got_ref[span]
        out_ref[share:] = tail


def ritz_kernel(scalar_ref, local_ref, own_ref, got_refs, wave_out, sigma_out, energy_out):
    scale, rayleigh, wave_corr, corr_sq, corr_resid, corr_sigma, wave_resid = (scalar_ref[i : i + 1, :1] for i in range(7))
    rows = own_ref.shape[1]
    got = got_refs[0][...]
    for ref in got_refs[1:]:
        got += ref[...]
    curve = got[2 * rows : 2 * rows + 1, :1]
    ops = lax.axis_index("ops")
    core = ops % 2
    span = pl.ds(pl.multiple_of(ops // 2 * (2 * rows), 2 * rows), 2 * rows)
    along = wave_corr / scale
    lift = along / scale
    norm_sq = corr_sq - along * along
    norm = jnp.sqrt(norm_sq)
    coupling = (corr_resid - lift * wave_resid) / norm
    curvature = (curve - 2.0 * lift * corr_sigma + along * along * rayleigh) / norm_sq
    half_gap = 0.5 * (curvature - rayleigh)
    radius = jnp.sqrt(half_gap * half_gap + coupling * coupling)
    energy = 0.5 * (rayleigh + curvature) - radius
    safe = jnp.where(radius > 0.0, radius, 1.0)
    big = jnp.sqrt(0.5 + 0.5 * (jnp.abs(half_gap) / safe))
    small = (0.5 * (jnp.abs(coupling) / safe)) / big
    ahead = half_gap >= 0.0
    cos_part = jnp.where(radius > 0.0, jnp.where(ahead, big, small), 1.0)
    sin_size = jnp.where(radius > 0.0, jnp.where(ahead, small, big), 0.0)
    sin_part = jnp.where(coupling < 0.0, sin_size, -sin_size)
    factor = sin_part * scale / norm
    for s in range(2):
        wave, sigma = rows_here(local_ref[s, span], core), own_ref[2 + s]
        wave_out[s] = cos_part * wave + factor * (own_ref[s] - lift * wave)
        sigma_out[s] = cos_part * sigma + factor * (got[s * rows : (s + 1) * rows] - lift * sigma)
    energy_out[...] = jnp.broadcast_to(energy, energy_out.shape)


def body(n_ops, n_sec, wavefunction, hamiltonian_diag, mirror_coupling, left_env, right_env, term_source):
    owned, size, _ = wavefunction.shape
    terms = left_env.shape[0]
    half = terms // 4 * 2
    chips = n_ops // 2
    rows = size // n_ops
    shape = jax.ShapeDtypeStruct

    def swap(values):
        return lax.ppermute(values, "ops", [(i, i ^ 1) for i in range(n_ops)])

    def to_chip(values, m):
        return lax.ppermute(values, "ops", [(i, i ^ (2 * m)) for i in range(n_ops)])

    def to_plane(values, m):
        return lax.ppermute(values, "sec", [(i, i ^ m) for i in range(n_sec)])

    def to_planes(values, pair):
        moves = [(o * n_sec + z, o * n_sec + (z ^ pair[o % 2])) for o in range(n_ops) for z in range(n_sec)]
        return lax.ppermute(values, ("ops", "sec"), moves)

    def gather_planes(values):
        return [values] + [to_plane(values, m) for m in range(1, n_sec)]

    matmul_flops = terms * owned * size * size * size * 12
    slot_shape = (2 * n_sec + 1, 2 * size, 2 * size)
    stack_shape = (owned * size, 2 * terms * size)
    half_shape = (owned * size, terms * size)
    message_shape = shape((size + PAD, size), F32)
    scalar_shape = shape((PAD, size), F32)

    def in_hbm(values):
        return pltpu.with_memory_space_constraint(values, pltpu.HBM)

    zs, last = partners(n_sec)

    with jax.named_scope("gather_wave"):
        mine = [to_planes(wavefunction, pair) for pair in zs]
        sectors = call(
            pack_kernel,
            (shape((size + size // chips, size), F32), shape((size, size), F32)),
            [HBM] * 2,
            [pltpu.SemaphoreType.DMA((3,))],
            limit=SMALL,
        )(in_hbm(wavefunction), in_hbm(hamiltonian_diag))
        mine.append(to_plane(sectors[0], last))
    with jax.named_scope("gather_diag"):
        diag = [to_planes(hamiltonian_diag, pair) for pair in zs]
    with jax.named_scope("load"):
        held = [left_env, right_env, wavefunction, term_source.T, mirror_coupling[None]]
        loaded = call(
            load_kernel,
            (
                shape((terms, owned, size, 2 * size), BF16),
                shape((2 * terms * size, 2 * size), BF16),
                *(shape(values.shape, values.dtype) for values in held[2:]),
            ),
            [HBM] * len(held),
            [
                pltpu.VMEM(left_env.shape, F32),
                pltpu.VMEM(right_env.shape, F32),
                pltpu.SemaphoreType.DMA((len(held),)),
            ],
            limit=SMALL,
        )(*[in_hbm(values) for values in held])
        loaded, mine[:-1] = lax.optimization_barrier((loaded, mine[:-1]))
        pairs, weights, local, source, coupling = loaded
    with jax.named_scope("swap_wave"):
        theirs = [swap(values) for values in mine]
        (*mine, last), (*theirs, other_last) = mine, theirs
    with jax.named_scope("first_apply"):
        keep, send, norm = call(
            functools.partial(first_kernel, n_sec, n_ops),
            (message_shape, message_shape, scalar_shape),
            [SMEM, VMEM] + [VMEM] * 3 + [[VMEM] * len(zs)] * 2 + [VMEM] * 2,
            [pltpu.VMEM(slot_shape, BF16), pltpu.VMEM(stack_shape, BF16)],
            matmul_flops,
        )(source, coupling, pairs, weights, local, mine, theirs, last, other_last)
    with jax.named_scope("reduce_sigma"):
        joined = call(
            join_kernel, shape((size + PAD + size // chips, size), F32), [VMEM] * 3, limit=SMALL
        )(keep, swap(send), last)
        summed, last_diag = call(
            plane_kernel, (message_shape, shape((size, size), F32)), [[VMEM] * chips], limit=SMALL
        )([joined] + [to_chip(joined, m) for m in range(1, chips)])
    with jax.named_scope("swap_diag"):
        other_diag = [
            swap(call(other_kernel, shape((size, size), F32), [VMEM], limit=SMALL)(values)) for values in diag
        ]
    with jax.named_scope("gather_sigma"):
        sums = gather_planes(summed)
    with jax.named_scope("correction"):
        found = call(
            functools.partial(correction_kernel, n_sec),
            shape(((n_sec + 1) * size + PAD, size), F32),
            [VMEM, [VMEM] * 2, [VMEM] * len(zs), [VMEM] * len(zs), [VMEM] * 2, [VMEM] * len(zs), [VMEM] * len(zs), [VMEM] * n_sec],
            limit=SMALL,
        )(norm, list(sectors), mine, theirs, [last, last_diag], diag, other_diag, sums)
        other = swap(found)
    with jax.named_scope("even_terms"):
        slots, part, curve, kept, scalars = call(
            functools.partial(even_kernel, n_sec, n_ops),
            (
                shape(slot_shape, BF16),
                shape((owned, size, size), F32),
                scalar_shape,
                shape((2 * owned, rows, size), F32),
                scalar_shape,
            ),
            [SMEM, VMEM] + [VMEM] * 4,
            [pltpu.VMEM(half_shape, BF16)],
            matmul_flops // 2,
        )(source, coupling, pairs, weights, found, other)
        curves = gather_planes(curve)
    with jax.named_scope("odd_terms"):
        keep, send = call(
            functools.partial(odd_kernel, n_sec, n_ops),
            (shape((size, size), F32), shape((size, size), F32)),
            [SMEM] + [VMEM] * 4,
            [pltpu.VMEM(half_shape, BF16)],
            matmul_flops // 2,
        )(source, pairs, weights, slots, part)
    with jax.named_scope("reduce_dir_sigma"):
        keep, send = call(curve_kernel, (message_shape, message_shape), [VMEM, VMEM, [VMEM] * n_sec], limit=SMALL)(
            keep, send, curves
        )
        dealt = call(deal_kernel, [shape((2 * rows + PAD, size), F32)] * chips, [VMEM, VMEM], limit=SMALL)(keep, swap(send))
        got = [dealt[0]] + [to_chip(dealt[m], m) for m in range(1, chips)]
    with jax.named_scope("ritz"):
        new_wave, new_sigma, energy = call(
            ritz_kernel,
            (shape((owned, rows, size), F32), shape((owned, rows, size), F32), shape((1, size), F32)),
            [VMEM] * 3 + [[VMEM] * chips],
        )(scalars, local, kept, got)
    return (new_wave, new_sigma, energy[0, :1])


def solution(mesh):
    placed = (
        P("sec", None, None),
        P("sec", None, None),
        P("sec"),
        P("ops", "sec", None, None),
        P("ops", None, None),
        P("ops", "sec"),
    )
    return jax.shard_map(
        functools.partial(body, mesh.shape["ops"], mesh.shape["sec"]),
        mesh=mesh,
        in_specs=placed,
        out_specs=(P("sec", "ops", None), P("sec", "ops", None), P()),
        check_vma=False,
    )
```

```python
import functools

import jax
import jax.numpy as jnp
from jax import lax
from jax.experimental import pallas as pl
from jax.experimental.pallas import tpu as pltpu
from jax.sharding import PartitionSpec as P

F32 = jnp.float32
BF16 = jnp.bfloat16
VMEM = pl.BlockSpec(memory_space=pltpu.VMEM)
HBM = pl.BlockSpec(memory_space=pltpu.HBM)
SMEM = pl.BlockSpec(memory_space=pltpu.SMEM)
PAD = 8
LIMIT = 16 * 1024 * 1024
SMALL = 16 * 1024 * 1024


def call(kernel, out_shape, in_specs, scratch=(), flops=0, limit=LIMIT):
    return pl.pallas_call(
        kernel,
        out_shape=out_shape,
        in_specs=in_specs,
        out_specs=jax.tree.map(lambda _: VMEM, out_shape),
        scratch_shapes=list(scratch),
        compiler_params=pltpu.CompilerParams(vmem_limit_bytes=limit),
        cost_estimate=pl.CostEstimate(flops=flops, bytes_accessed=1 << 20, transcendentals=0),
    )


def split(values):
    high = values.astype(BF16)
    return high, (values - high.astype(F32)).astype(BF16)


def total(values):
    return jnp.sum(values, keepdims=True)


def spread(value, size):
    return jnp.broadcast_to(value, (1, size))


def position(k, terms):
    return k // 2 + k % 2 * (terms // 2)


def load_kernel(left_ref, right_ref, wave_ref, source_ref, coupling_ref,
                pairs_ref, weights_ref, local_ref, sources_ref, couplings_ref, left_buf, right_buf, sems):
    terms, owned, size, _ = left_ref.shape
    sources = (left_ref, right_ref, wave_ref, source_ref, coupling_ref)
    targets = (left_buf, right_buf, local_ref, sources_ref, couplings_ref)
    copies = [pltpu.make_async_copy(source, target, sems.at[i]) for i, (source, target) in enumerate(zip(sources, targets))]
    for copy in copies:
        copy.start()
    for copy in copies:
        copy.wait()
    for k in range(terms):
        for s in range(owned):
            pairs_ref[k, s, :, :size], pairs_ref[k, s, :, size:] = split(left_buf[k, s])
        base = 2 * size * position(k, terms)
        high, low = split(right_buf[k ^ 1])
        weights_ref[base : base + size, :size] = high
        weights_ref[base : base + size, size:] = low
        weights_ref[base + size : base + 2 * size, :size] = high
        weights_ref[base + size : base + 2 * size, size:] = jnp.zeros_like(high)


def pack_kernel(wave_ref, diag_ref, packed_ref, own_diag_ref, sems):
    owned, size, _ = wave_ref.shape
    share = packed_ref.shape[0] - owned * size
    ops = lax.axis_index("ops")
    core, chip = ops % 2, ops // 2
    rows = pl.ds(pl.multiple_of(chip * share, share), share)
    moves = [
        *((wave_ref.at[s], packed_ref.at[pl.ds(s * size, size)]) for s in range(owned)),
        (diag_ref.at[core, rows], packed_ref.at[pl.ds(owned * size, share)]),
        (diag_ref.at[core], own_diag_ref),
    ]
    copies = [pltpu.make_async_copy(source, target, sems.at[i]) for i, (source, target) in enumerate(moves)]
    for copy in copies:
        copy.start()
    for copy in copies:
        copy.wait()


def other_kernel(source_ref, target_ref):
    target_ref[...] = source_ref[1 - lax.axis_index("ops") % 2]


def partners(n_sec):
    return [(m, m + 1) for m in range(2, n_sec, 2)], 1


def from_partner(n_sec, m, core, mine, theirs, last):
    for i, pair in enumerate(partners(n_sec)[0]):
        if m in pair:
            return jnp.where(core == pair.index(m), mine(i), theirs(i))
    return last()


def store_vector(slots, at, block):
    size = block.shape[0]
    high, low = split(block)
    slots[at, :size, :size] = high
    slots[at, :size, size:] = low
    slots[at, size:, :size] = high
    slots[at, size:, size:] = jnp.zeros_like(high)


def apply_terms(chosen, n_sec, source_ref, pairs_ref, weights_ref, slots, stacked):
    terms, owned, size, _ = pairs_ref.shape
    plane = lax.axis_index("sec")
    first = position(chosen[0], terms)
    for k in chosen:
        base = 2 * size * (position(k, terms) - first)
        for s in range(owned):
            source = source_ref[s, k]
            at = 2 * jnp.bitwise_xor(source // 2, plane) + jnp.bitwise_and(source, 1)
            inner = jnp.dot(pairs_ref[k, s], slots[jnp.where(source < 0, 2 * n_sec, at)], preferred_element_type=F32)
            high, low = split(inner[:, :size] + inner[:, size:])
            stacked[s * size : (s + 1) * size, base : base + size] = high
            stacked[s * size : (s + 1) * size, base + size : base + 2 * size] = low
    span = pl.ds(2 * size * first, 2 * size * len(chosen))
    both = jnp.dot(stacked[...], weights_ref[span], preferred_element_type=F32)
    return both[:, :size] + both[:, size:]


def join_kernel(keep_ref, got_ref, last_ref, out_ref):
    rows, size = keep_ref.shape
    out_ref[:rows] = keep_ref[...] + got_ref[...]
    out_ref[rows:] = last_ref[2 * size :]


def plane_kernel(part_refs, sum_ref, diag_ref):
    rows = sum_ref.shape[0]
    summed = part_refs[0][:rows]
    for ref in part_refs[1:]:
        summed += ref[:rows]
    sum_ref[...] = summed
    chip = lax.axis_index("ops") // 2
    share = diag_ref.shape[0] // len(part_refs)
    for m, ref in enumerate(part_refs):
        first = pl.multiple_of(jnp.bitwise_xor(chip, m) * share, share)
        diag_ref[pl.ds(first, share)] = ref[rows:]


def first_kernel(n_sec, n_ops, source_ref, coupling_ref, pairs_ref, weights_ref, local_ref, mine_refs, theirs_refs,
                 last_ref, keep_ref, send_ref, norm_ref, slots, stacked):
    size = local_ref.shape[1]
    core = lax.axis_index("ops") % 2
    pairs, last = partners(n_sec)
    blocks = [(s, local_ref[s]) for s in range(2)]
    for i, (even, odd) in enumerate(pairs):
        for refs, m in ((mine_refs, jnp.where(core == 0, even, odd)), (theirs_refs, jnp.where(core == 0, odd, even))):
            blocks += [(2 * m + s, refs[i][s]) for s in range(2)]
    blocks += [(2 * last + s, last_ref[s * size : (s + 1) * size]) for s in range(2)]
    acc = jnp.zeros((size, size), F32)
    for at, block in blocks:
        acc += block * block
        store_vector(slots, at, block)
    slots[2 * n_sec] = jnp.zeros_like(slots[2 * n_sec])
    norm_ref[...] = jnp.broadcast_to(total(acc), norm_ref.shape)
    part = apply_terms(range(pairs_ref.shape[0]), n_sec, source_ref, pairs_ref, weights_ref, slots, stacked)
    corr = jnp.zeros((1, 1), F32)
    blocks = []
    for s in range(2):
        partner = from_partner(
            n_sec, n_sec // 2, core, lambda i: mine_refs[i][s], lambda i: theirs_refs[i][s],
            lambda: last_ref[s * size : (s + 1) * size],
        )
        blocks.append(part[s * size : (s + 1) * size] + (coupling_ref[0, s] / n_ops) * partner.T)
        corr += total(local_ref[s] * blocks[s])
    keep_ref[:size] = jnp.where(core == 0, blocks[0], blocks[1])
    send_ref[:size] = jnp.where(core == 0, blocks[1], blocks[0])
    keep_ref[size:] = jnp.broadcast_to(corr, (PAD, size))
    send_ref[size:] = jnp.broadcast_to(corr, (PAD, size))


def correction_kernel(n_sec, norm_ref, sector_refs, mine_refs, theirs_refs, last_refs, diag_refs, other_diag_refs, sum_refs, out_ref):
    size = sector_refs[1].shape[0]
    core = lax.axis_index("ops") % 2
    sector = pl.ds(pl.multiple_of(core * size, size), size)
    norm_sq = norm_ref[:1, :1]
    corr = sum_refs[0][size : size + 1, :1]
    for ref in sum_refs[1:]:
        corr += ref[size : size + 1, :1]
    scale = jnp.sqrt(norm_sq)
    inverse = 1.0 / scale
    rayleigh = corr / norm_sq
    sums = [jnp.zeros((size, size), F32) for _ in range(5)]
    for m in range(n_sec):
        if m == 0:
            wave, diag = sector_refs[0][sector], sector_refs[1][...]
        else:
            wave = from_partner(
                n_sec, m, core, lambda i: mine_refs[i][core], lambda i: theirs_refs[i][core], lambda: last_refs[0][sector]
            )
            diag = from_partner(
                n_sec, m, core, lambda i: diag_refs[i][core], lambda i: other_diag_refs[i][...], lambda: last_refs[1][...]
            )
        sigma = sum_refs[m][:size]
        resid = sigma * inverse - rayleigh * (wave * inverse)
        offset = diag - rayleigh
        corrected = resid / (1.0 + offset * offset)
        out_ref[m * size : (m + 1) * size] = corrected
        for i, factor in enumerate((wave, corrected, resid, sigma)):
            sums[i] += corrected * factor
        sums[4] += wave * resid
    out_ref[n_sec * size : (n_sec + 1) * size] = sum_refs[0][:size]
    tail = [spread(scale, size), spread(rayleigh, size)] + [spread(total(values), size) for values in sums]
    for i, row in enumerate(tail):
        out_ref[(n_sec + 1) * size + i : (n_sec + 1) * size + i + 1] = row
    for i in range(len(tail), PAD):
        out_ref[(n_sec + 1) * size + i : (n_sec + 1) * size + i + 1] = jnp.zeros((1, size), F32)


def rows_here(block, core):
    rows = block.shape[0] // 2
    return jnp.where(core == 0, block[:rows], block[rows:])


def even_kernel(n_sec, n_ops, source_ref, coupling_ref, pairs_ref, weights_ref, mine_ref, theirs_ref,
                slots, part_ref, curve_ref, own_ref, scalar_ref, stacked):
    size = pairs_ref.shape[2]
    core = lax.axis_index("ops") % 2
    for m in range(n_sec):
        span = pl.ds(m * size, size)
        store_vector(slots, 2 * m + core, mine_ref[span])
        store_vector(slots, 2 * m + 1 - core, theirs_ref[span])
    slots[2 * n_sec] = jnp.zeros_like(slots[2 * n_sec])
    part = apply_terms(range(0, pairs_ref.shape[0], 2), n_sec, source_ref, pairs_ref, weights_ref, slots, stacked)
    curve = jnp.zeros((1, 1), F32)
    mirror = pl.ds(n_sec // 2 * size, size)
    chip = lax.axis_index("ops") // 2
    share = 2 * own_ref.shape[1]
    for s in range(2):
        mine = core == s
        vec = jnp.where(mine, mine_ref[:size], theirs_ref[:size])
        partner = jnp.where(mine, mine_ref[mirror], theirs_ref[mirror])
        block = part[s * size : (s + 1) * size]
        mirrored = (coupling_ref[0, s] / n_ops) * partner.T
        part_ref[s] = block + mirrored
        for i, first in enumerate((0, n_sec)):
            span = pl.ds(pl.multiple_of(first * size + chip * share, share), share)
            own_ref[2 * i + s] = rows_here(jnp.where(mine, mine_ref[span], theirs_ref[span]), core)
        curve += total(vec * (2.0 * block + mirrored))
    curve_ref[...] = jnp.broadcast_to(curve, curve_ref.shape)
    tail = pl.ds((n_sec + 1) * size, PAD)
    row = lax.broadcasted_iota(jnp.int32, (PAD, size), 0)
    scalar_ref[...] = mine_ref[tail] + jnp.where(row < 2, 0.0, theirs_ref[tail])


def odd_kernel(n_sec, n_ops, source_ref, pairs_ref, weights_ref, slots, part_ref, keep_ref, send_ref, stacked):
    size = pairs_ref.shape[2]
    core = lax.axis_index("ops") % 2
    part = apply_terms(range(1, pairs_ref.shape[0], 2), n_sec, source_ref, pairs_ref, weights_ref, slots, stacked)
    rows = size // n_ops
    for s in range(2):
        block = part[s * size : (s + 1) * size] + part_ref[s]
        for q in range(n_ops // 2):
            at_row = (q * 2 + s) * rows
            even = block[2 * q * rows : (2 * q + 1) * rows]
            odd = block[(2 * q + 1) * rows : (2 * q + 2) * rows]
            keep_ref[at_row : at_row + rows] = jnp.where(core == 0, even, odd)
            send_ref[at_row : at_row + rows] = jnp.where(core == 0, odd, even)


def curve_kernel(keep_ref, send_ref, curve_refs, keep_out, send_out):
    size = keep_ref.shape[0]
    curve = curve_refs[0][...]
    for ref in curve_refs[1:]:
        curve += ref[...]
    for ref, out in ((keep_ref, keep_out), (send_ref, send_out)):
        out[:size] = ref[...]
        out[size:] = curve


def deal_kernel(keep_ref, got_ref, *out_refs):
    share = out_refs[0].shape[0] - PAD
    size = keep_ref.shape[0] - PAD
    chip = lax.axis_index("ops") // 2
    tail = keep_ref[size:] + got_ref[size:]
    for m, out_ref in enumerate(out_refs):
        span = pl.ds(pl.multiple_of(jnp.bitwise_xor(chip, m) * share, share), share)
        out_ref[:share] = keep_ref[span] + got_ref[span]
        out_ref[share:] = tail


def ritz_kernel(scalar_ref, local_ref, own_ref, got_refs, wave_out, sigma_out, energy_out):
    scale, rayleigh, wave_corr, corr_sq, corr_resid, corr_sigma, wave_resid = (scalar_ref[i : i + 1, :1] for i in range(7))
    rows = own_ref.shape[1]
    got = got_refs[0][...]
    for ref in got_refs[1:]:
        got += ref[...]
    curve = got[2 * rows : 2 * rows + 1, :1]
    ops = lax.axis_index("ops")
    core = ops % 2
    span = pl.ds(pl.multiple_of(ops // 2 * (2 * rows), 2 * rows), 2 * rows)
    along = wave_corr / scale
    lift = along / scale
    norm_sq = corr_sq - along * along
    norm = jnp.sqrt(norm_sq)
    coupling = (corr_resid - lift * wave_resid) / norm
    curvature = (curve - 2.0 * lift * corr_sigma + along * along * rayleigh) / norm_sq
    half_gap = 0.5 * (curvature - rayleigh)
    radius = jnp.sqrt(half_gap * half_gap + coupling * coupling)
    energy = 0.5 * (rayleigh + curvature) - radius
    safe = jnp.where(radius > 0.0, radius, 1.0)
    big = jnp.sqrt(0.5 + 0.5 * (jnp.abs(half_gap) / safe))
    small = (0.5 * (jnp.abs(coupling) / safe)) / big
    ahead = half_gap >= 0.0
    cos_part = jnp.where(radius > 0.0, jnp.where(ahead, big, small), 1.0)
    sin_size = jnp.where(radius > 0.0, jnp.where(ahead, small, big), 0.0)
    sin_part = jnp.where(coupling < 0.0, sin_size, -sin_size)
    factor = sin_part * scale / norm
    for s in range(2):
        wave, sigma = rows_here(local_ref[s, span], core), own_ref[2 + s]
        wave_out[s] = cos_part * wave + factor * (own_ref[s] - lift * wave)
        sigma_out[s] = cos_part * sigma + factor * (got[s * rows : (s + 1) * rows] - lift * sigma)
    energy_out[...] = jnp.broadcast_to(energy, energy_out.shape)


def body(n_ops, n_sec, wavefunction, hamiltonian_diag, mirror_coupling, left_env, right_env, term_source):
    owned, size, _ = wavefunction.shape
    terms = left_env.shape[0]
    half = terms // 4 * 2
    chips = n_ops // 2
    rows = size // n_ops
    shape = jax.ShapeDtypeStruct

    def swap(values):
        return lax.ppermute(values, "ops", [(i, i ^ 1) for i in range(n_ops)])

    def to_chip(values, m):
        return lax.ppermute(values, "ops", [(i, i ^ (2 * m)) for i in range(n_ops)])

    def to_plane(values, m):
        return lax.ppermute(values, "sec", [(i, i ^ m) for i in range(n_sec)])

    def to_planes(values, pair):
        moves = [(o * n_sec + z, o * n_sec + (z ^ pair[o % 2])) for o in range(n_ops) for z in range(n_sec)]
        return lax.ppermute(values, ("ops", "sec"), moves)

    def gather_planes(values):
        return [values] + [to_plane(values, m) for m in range(1, n_sec)]

    matmul_flops = terms * owned * size * size * size * 12
    slot_shape = (2 * n_sec + 1, 2 * size, 2 * size)
    stack_shape = (owned * size, 2 * terms * size)
    half_shape = (owned * size, terms * size)
    message_shape = shape((size + PAD, size), F32)
    scalar_shape = shape((PAD, size), F32)

    def in_hbm(values):
        return pltpu.with_memory_space_constraint(values, pltpu.HBM)

    zs, last = partners(n_sec)

    with jax.named_scope("gather_wave"):
        mine = [to_planes(wavefunction, pair) for pair in zs]
        sectors = call(
            pack_kernel,
            (shape((owned * size + size // chips, size), F32), shape((size, size), F32)),
            [HBM] * 2,
            [pltpu.SemaphoreType.DMA((owned + 2,))],
            limit=SMALL,
        )(in_hbm(wavefunction), in_hbm(hamiltonian_diag))
        mine.append(to_plane(sectors[0], last))
    with jax.named_scope("gather_diag"):
        diag = [to_planes(hamiltonian_diag, pair) for pair in zs]
    with jax.named_scope("load"):
        held = [left_env, right_env, wavefunction, term_source.T, mirror_coupling[None]]
        loaded = call(
            load_kernel,
            (
                shape((terms, owned, size, 2 * size), BF16),
                shape((2 * terms * size, 2 * size), BF16),
                *(shape(values.shape, values.dtype) for values in held[2:]),
            ),
            [HBM] * len(held),
            [
                pltpu.VMEM(left_env.shape, F32),
                pltpu.VMEM(right_env.shape, F32),
                pltpu.SemaphoreType.DMA((len(held),)),
            ],
            limit=SMALL,
        )(*[in_hbm(values) for values in held])
        loaded, mine[:-1] = lax.optimization_barrier((loaded, mine[:-1]))
        pairs, weights, local, source, coupling = loaded
    with jax.named_scope("swap_wave"):
        *mine, last = mine
        theirs = [swap(values) for values in mine]
    with jax.named_scope("first_apply"):
        keep, send, norm = call(
            functools.partial(first_kernel, n_sec, n_ops),
            (message_shape, message_shape, scalar_shape),
            [SMEM, SMEM] + [VMEM] * 3 + [[VMEM] * len(zs)] * 2 + [VMEM],
            [pltpu.VMEM(slot_shape, BF16), pltpu.VMEM(stack_shape, BF16)],
            matmul_flops,
        )(source, coupling, pairs, weights, local, mine, theirs, last)
    with jax.named_scope("reduce_sigma"):
        joined = call(
            join_kernel, shape((size + PAD + size // chips, size), F32), [VMEM] * 3, limit=SMALL
        )(keep, swap(send), last)
        summed, last_diag = call(
            plane_kernel, (message_shape, shape((size, size), F32)), [[VMEM] * chips], limit=SMALL
        )([joined] + [to_chip(joined, m) for m in range(1, chips)])
    with jax.named_scope("swap_diag"):
        other_diag = [
            swap(call(other_kernel, shape((size, size), F32), [VMEM], limit=SMALL)(values)) for values in diag
        ]
    with jax.named_scope("gather_sigma"):
        sums = gather_planes(summed)
    with jax.named_scope("correction"):
        found = call(
            functools.partial(correction_kernel, n_sec),
            shape(((n_sec + 1) * size + PAD, size), F32),
            [VMEM, [VMEM] * 2, [VMEM] * len(zs), [VMEM] * len(zs), [VMEM] * 2, [VMEM] * len(zs), [VMEM] * len(zs), [VMEM] * n_sec],
            limit=SMALL,
        )(norm, list(sectors), mine, theirs, [last, last_diag], diag, other_diag, sums)
        other = swap(found)
    with jax.named_scope("even_terms"):
        slots, part, curve, kept, scalars = call(
            functools.partial(even_kernel, n_sec, n_ops),
            (
                shape(slot_shape, BF16),
                shape((owned, size, size), F32),
                scalar_shape,
                shape((2 * owned, rows, size), F32),
                scalar_shape,
            ),
            [SMEM, SMEM] + [VMEM] * 4,
            [pltpu.VMEM(half_shape, BF16)],
            matmul_flops // 2,
        )(source, coupling, pairs, weights, found, other)
        curves = gather_planes(curve)
    with jax.named_scope("odd_terms"):
        keep, send = call(
            functools.partial(odd_kernel, n_sec, n_ops),
            (shape((size, size), F32), shape((size, size), F32)),
            [SMEM] + [VMEM] * 4,
            [pltpu.VMEM(half_shape, BF16)],
            matmul_flops // 2,
        )(source, pairs, weights, slots, part)
    with jax.named_scope("reduce_dir_sigma"):
        keep, send = call(curve_kernel, (message_shape, message_shape), [VMEM, VMEM, [VMEM] * n_sec], limit=SMALL)(
            keep, send, curves
        )
        dealt = call(deal_kernel, [shape((2 * rows + PAD, size), F32)] * chips, [VMEM, VMEM], limit=SMALL)(keep, swap(send))
        got = [dealt[0]] + [to_chip(dealt[m], m) for m in range(1, chips)]
    with jax.named_scope("ritz"):
        new_wave, new_sigma, energy = call(
            ritz_kernel,
            (shape((owned, rows, size), F32), shape((owned, rows, size), F32), shape((1, size), F32)),
            [VMEM] * 3 + [[VMEM] * chips],
        )(scalars, local, kept, got)
    return (new_wave, new_sigma, energy[0, :1])


def solution(mesh):
    placed = (
        P("sec", None, None),
        P("sec", None, None),
        P("sec"),
        P("ops", "sec", None, None),
        P("ops", None, None),
        P("ops", "sec"),
    )
    return jax.shard_map(
        functools.partial(body, mesh.shape["ops"], mesh.shape["sec"]),
        mesh=mesh,
        in_specs=placed,
        out_specs=(P("sec", "ops", None), P("sec", "ops", None), P()),
        check_vma=False,
    )
```
